32 devices in a mesh: groups: 2 (over y), expert: 4 (over z), dp: 4 (over x, core).
Axes of the slice: x: 2, y: 2, z: 4, core: 2. Of those that a mesh axis runs over, the one named last changes fastest.
Arguments:
- tokens: bfloat16 [384, 6144], P(('groups', 'expert'), 'dp'), parts along dimension 0, may hold values from -6 to 6
- expert_ids: int32 [384, 2], P(('groups', 'expert')), parts along dimension 0, may hold values from 0 to 7, as said below
- route_weights: float32 [384, 2], P(('groups', 'expert')), parts along dimension 0, may hold values from 0.1 to 0.9
- gate_weight: bfloat16 [6144, 16384], P('dp', 'expert'), may hold values from -0.078125 to 0.078125
- up_weight: bfloat16 [6144, 16384], P('dp', 'expert'), may hold values from -0.078125 to 0.078125
- down_weight: bfloat16 [16384, 6144], P('expert', 'dp'), may hold values from -0.0625 to 0.0625
- gate_probe: bfloat16 [6144, 16384], P('dp', 'expert'), may hold values from -1 to 1, as said below
- up_probe: bfloat16 [6144, 16384], P('dp', 'expert'), may hold values from -1 to 1, as said below
Outputs:
- gate_hvp: bfloat16 [12288, 16384], P(('groups', 'dp'), 'expert'), parts along dimension 0
- up_hvp: bfloat16 [12288, 16384], P(('groups', 'dp'), 'expert'), parts along dimension 0
The draws below stay inside these ranges and needn't reach their ends.
There are 2 independent parts, one for each index of `groups`. The reference program is written for one: setup_inputs(seed, part) draws one part's arguments, and reference() takes and returns one part's arrays. A program takes and returns all parts, laid end to end along the dimension named above; an argument that names none is the same for every part. Nothing has to cross between parts.
Inputs may be any that keep to these rules, and one draw needn't show every extreme that they name: `expert_ids`: A row never names one expert twice. Among the 48 rows of one index of expert, each window expert below 2 is named by at most 24 rows, and one of them is named by exactly 24 rows in every such block. `gate_probe`: every entry is +1 or -1. `up_probe`: every entry is +1 or -1.
All inputs are finite; a program needn't handle non-finite values.
Results may differ from the reference program's by a relative error of at most 0.025.
Values may be sent and summed in bfloat16 or wider, within the bound.
No kernel may reach another device: no remote copies, remote signals or barrier semaphores. Data moves between devices by JAX's collectives and lax.ppermute only.
A program may use at most 192 MiB of HBM per device.

```python
import jax
import jax.numpy as jnp
from jax import lax

D = 6144
HID = 8192
ROUTED = 8
EXPERTS = 2
TOK_DEV = 48
CAP = 24
TOKENS = 192
BLOCK = 4096
FEAT = 1536
N_DP = 4


def draw_expert_ids(key, part):
    key = jax.random.fold_in(key, 7)
    key_list = jax.random.split(key, 6)
    block_count = TOKENS // TOK_DEV
    hot_expert = jax.random.randint(key_list[0], (), 0, EXPERTS)
    block_keys = jax.random.split(key_list[1], block_count)
    row_order = jax.vmap(lambda sub_key: jax.random.permutation(sub_key, TOK_DEV))(block_keys)
    hot_rows = jnp.argsort(row_order, axis=1) < CAP
    first_raw = jax.random.randint(key_list[2], (block_count, TOK_DEV), 0, ROUTED - 1)
    first_pick = first_raw + (first_raw >= hot_expert).astype(jnp.int32)
    second_raw = jax.random.randint(key_list[3], (block_count, TOK_DEV), 0, ROUTED - 2)
    low_pick = jnp.minimum(first_pick, hot_expert)
    high_pick = jnp.maximum(first_pick, hot_expert)
    second = second_raw + (second_raw >= low_pick).astype(jnp.int32)
    second = second + (second >= high_pick).astype(jnp.int32)
    hot_second = jax.random.randint(key_list[4], (block_count, TOK_DEV), EXPERTS, ROUTED)
    column_one = jnp.where(hot_rows, hot_expert, first_pick)
    column_two = jnp.where(hot_rows, hot_second, second)
    column_flip = jax.random.randint(key_list[5], (block_count, TOK_DEV), 0, 2) == 1
    left_col = jnp.where(column_flip, column_two, column_one)
    right_col = jnp.where(column_flip, column_one, column_two)
    return jnp.stack([left_col, right_col], axis=-1).reshape(TOKENS, 2).astype(jnp.int32)


def draw_gate_probe(key, part):
    key = jax.random.fold_in(key, 3)
    return jax.random.rademacher(key, (D, EXPERTS * HID), dtype=jnp.float32).astype(jnp.bfloat16)


def draw_up_probe(key, part):
    key = jax.random.fold_in(key, 5)
    return jax.random.rademacher(key, (D, EXPERTS * HID), dtype=jnp.float32).astype(jnp.bfloat16)


def level_of(rng, extent, cuts, least, largest):
    def one(position, parts):
        draws = jax.random.uniform(jax.random.fold_in(jax.random.fold_in(rng, 6), position), (parts,), jnp.float32, least / len(cuts), largest / len(cuts))
        return jnp.repeat(jnp.exp(draws), extent[position] // parts).reshape((-1,) + (1,) * (len(extent) - position - 1))

    loudness = one(*cuts[0])
    for cut in cuts[1:]:
        loudness = loudness * one(*cut)
    return loudness


def normal_values(rng, dims, scale, bound, shards=(), held_as=jnp.bfloat16):
    result = jax.random.normal(rng, dims, jnp.float32) * scale
    if len(shards) > 0:
        result = level_of(rng, dims, shards, -0.22, 0.18) * result
    return jnp.clip(result, min=-bound, max=bound).astype(held_as)


def setup_inputs(seed: int = 0, part: int = 0) -> dict:
    splits = jax.random.split(jax.random.key(seed), 9)
    part_splits = jax.random.split(jax.random.fold_in(splits[8], part), 9)
    tokens = normal_values(part_splits[0], (TOKENS, D), 1.0, 6.0, ((0, 4), (1, 4)))
    expert_ids = draw_expert_ids(jax.random.fold_in(jax.random.fold_in(splits[8], part), 71), part)
    route_weights = jnp.clip(0.1 + 0.79999997 * jax.random.uniform(part_splits[2], (TOKENS, 2), jnp.float32) ** level_of(part_splits[2], (TOKENS, 2), ((0, 4),), -0.2, 0.2), 0.1, 0.9)
    gate_weight = normal_values(splits[3], (D, EXPERTS * HID), D ** -0.5, 0.078125, ((0, 4), (1, 4)))
    up_weight = normal_values(splits[4], (D, EXPERTS * HID), D ** -0.5, 0.078125, ((0, 4), (1, 4)))
    down_weight = normal_values(splits[5], (EXPERTS * HID, D), HID ** -0.5, 0.0625, ((0, 4), (1, 4)))
    gate_probe = draw_gate_probe(jax.random.fold_in(splits[8], 71), part)
    up_probe = draw_up_probe(jax.random.fold_in(splits[8], 71), part)
    return dict(tokens=tokens, expert_ids=expert_ids, route_weights=route_weights, gate_weight=gate_weight, up_weight=up_weight, down_weight=down_weight, gate_probe=gate_probe, up_probe=up_probe)


def sigmoid_terms(gate_value):
    sigmoid_value = jax.nn.sigmoid(gate_value)
    active = gate_value * sigmoid_value
    slope_value = sigmoid_value + gate_value * sigmoid_value * (1.0 - sigmoid_value)
    bend_value = sigmoid_value * (1.0 - sigmoid_value) * (2.0 + gate_value * (1.0 - 2.0 * sigmoid_value))
    return active, slope_value, bend_value


def forward_hidden(gate_value, up_value, gate_tangent, up_tangent):
    active, slope_value, bend_value = sigmoid_terms(gate_value)
    hidden = (active * up_value).astype(jnp.bfloat16)
    hidden_tangent = (slope_value * gate_tangent * up_value + active * up_tangent).astype(jnp.bfloat16)
    return hidden, hidden_tangent


def backward_terms(gate_value, up_value, gate_tangent, up_tangent, back_value, back_tangent):
    active, slope_value, bend_value = sigmoid_terms(gate_value)
    gate_term = (back_tangent * up_value * slope_value + back_value * up_tangent * slope_value
                 + back_value * up_value * bend_value * gate_tangent).astype(jnp.bfloat16)
    up_term = (back_tangent * active + back_value * slope_value * gate_tangent).astype(jnp.bfloat16)
    return gate_term, up_term


def split_product(left, right):
    row_count = left.shape[0]
    left_blocks = left.reshape(row_count, N_DP, FEAT).astype(jnp.float32)
    right_blocks = right.reshape(N_DP, FEAT, right.shape[1]).astype(jnp.float32)
    pieces = jnp.einsum("rnf,nfh->nrh", left_blocks, right_blocks)
    rounded = lax.optimization_barrier(pieces.astype(jnp.bfloat16))
    return jnp.sum(rounded.astype(jnp.float32), axis=0)


def split_back(left, down_rows):
    row_count = left.shape[0]
    left_blocks = left.reshape(row_count, N_DP, FEAT).astype(jnp.float32)
    down_blocks = down_rows.reshape(down_rows.shape[0], N_DP, FEAT).astype(jnp.float32)
    pieces = jnp.einsum("rnf,hnf->nrh", left_blocks, down_blocks)
    rounded = lax.optimization_barrier(pieces.astype(jnp.bfloat16))
    return jnp.sum(rounded.astype(jnp.float32), axis=0)


def block_outputs(hidden, hidden_tangent, down_rows):
    block_count = HID // BLOCK
    hidden_blocks = hidden.reshape(TOKENS, block_count, BLOCK).transpose(1, 0, 2)
    tangent_blocks = hidden_tangent.reshape(TOKENS, block_count, BLOCK).transpose(1, 0, 2)
    down_blocks = down_rows.reshape(block_count, BLOCK, D)

    def add_block(carry, pieces):
        hidden_piece, tangent_piece, down_piece = pieces
        value = jnp.dot(hidden_piece, down_piece, preferred_element_type=jnp.float32)
        tangent = jnp.dot(tangent_piece, down_piece, preferred_element_type=jnp.float32)
        value = lax.optimization_barrier(value.astype(jnp.bfloat16)).astype(jnp.float32)
        tangent = lax.optimization_barrier(tangent.astype(jnp.bfloat16)).astype(jnp.float32)
        return (carry[0] + value, carry[1] + tangent), None

    start = (jnp.zeros((TOKENS, D), jnp.float32), jnp.zeros((TOKENS, D), jnp.float32))
    totals, unused = lax.scan(add_block, start, (hidden_blocks, tangent_blocks, down_blocks))
    return totals


def reference(tokens, expert_ids, route_weights, gate_weight, up_weight, down_weight, gate_probe, up_probe):
    mixed = jnp.zeros((TOKENS, D), jnp.float32)
    mixed_tangent = jnp.zeros((TOKENS, D), jnp.float32)
    saved = []
    for expert in range(EXPERTS):
        low_col = expert * HID
        high_col = low_col + HID
        route_share = jnp.sum(jnp.where(expert_ids == expert, route_weights, jnp.float32(0.0)), axis=1)
        gate_value = split_product(tokens, gate_weight[:, low_col:high_col])
        up_value = split_product(tokens, up_weight[:, low_col:high_col])
        gate_tangent = split_product(tokens, gate_probe[:, low_col:high_col])
        up_tangent = split_product(tokens, up_probe[:, low_col:high_col])
        hidden, hidden_tangent = forward_hidden(gate_value, up_value, gate_tangent, up_tangent)
        down_rows = down_weight[low_col:high_col]
        out_sum, out_tangent_sum = block_outputs(hidden, hidden_tangent, down_rows)
        mixed = mixed + route_share[:, None] * out_sum
        mixed_tangent = mixed_tangent + route_share[:, None] * out_tangent_sum
        saved.append((route_share, gate_value, up_value, gate_tangent, up_tangent, down_rows))
    gate_cols = []
    up_cols = []
    for expert in range(EXPERTS):
        route_share, gate_value, up_value, gate_tangent, up_tangent, down_rows = saved[expert]
        cotangent = (route_share[:, None] * mixed / TOKENS).astype(jnp.bfloat16)
        cot_tangent = (route_share[:, None] * mixed_tangent / TOKENS).astype(jnp.bfloat16)
        back_value = split_back(cotangent, down_rows)
        back_tangent = split_back(cot_tangent, down_rows)
        gate_term, up_term = backward_terms(gate_value, up_value, gate_tangent, up_tangent, back_value, back_tangent)
        gate_cols.append(jnp.dot(tokens.T, gate_term, preferred_element_type=jnp.float32).astype(jnp.bfloat16))
        up_cols.append(jnp.dot(tokens.T, up_term, preferred_element_type=jnp.float32).astype(jnp.bfloat16))
    return jnp.concatenate(gate_cols, axis=1), jnp.concatenate(up_cols, axis=1)
```

```python
import functools

import jax
import jax.numpy as jnp
from jax import lax
from jax.experimental import pallas as pl
from jax.experimental.pallas import tpu as pltpu
from jax.sharding import PartitionSpec as P

EXPERTS = 2
BF16 = jnp.bfloat16
F32 = jnp.float32
KIB = 1024
MIB = 1024 * KIB
IN_VMEM = pl.BlockSpec(memory_space=pltpu.VMEM)
IN_SMEM = pl.BlockSpec(memory_space=pltpu.SMEM)
IN_HBM = pl.BlockSpec(memory_space=pltpu.HBM)
ANYWHERE = pl.BlockSpec(memory_space=pl.ANY)
SLOTS = 4


def swap(value, axis, mask):
    size = lax.axis_size(axis)
    return lax.ppermute(value, axis, [(i, i ^ mask) for i in range(size)])


def sub_width(width):
    return 512 if width % 512 == 0 else width


def params(limit):
    return pltpu.CompilerParams(vmem_limit_bytes=limit)


def cost(flops, size):
    return pl.CostEstimate(flops=flops, bytes_accessed=size, transcendentals=0)


def stream_kernel(count, offsets, me_ref, rows_ref, *refs):
    weights, outs, (slots_ref, sems) = refs[:count], refs[-4:-2], refs[-2:]
    quarter = outs[0].shape[2]
    slots, unused, sub = slots_ref.shape
    copies, targets = [], []
    for k in range(count):
        for out_ref, offset in zip(outs, offsets):
            base = (me_ref[0] ^ offset) * quarter
            for c in range(0, quarter, sub):
                columns = pl.ds(pl.multiple_of(base + c, sub), sub)
                slot = len(copies) % slots
                copies.append(
                    pltpu.make_async_copy(
                        weights[k].at[:, columns], slots_ref.at[slot], sems.at[slot]
                    )
                )
                targets.append(out_ref.at[k, :, c : c + sub])
    for copy in copies[:slots]:
        copy.start()
    for i, target_ref in enumerate(targets):
        copies[i].wait()
        target_ref[...] = jnp.dot(
            rows_ref[...], slots_ref[i % slots], preferred_element_type=F32
        ).astype(BF16)
        if i + slots < len(copies):
            copies[i + slots].start()


def quarter_products(me, rows, weights, offsets, after=()):
    count, (height, depth) = len(weights), rows.shape
    quarter = weights[0].shape[1] // 4
    sub = sub_width(quarter)
    slots = min(4, 2 * count * (quarter // sub))
    result = jax.ShapeDtypeStruct((count, height, quarter), BF16)
    return pl.pallas_call(
        functools.partial(stream_kernel, count, offsets),
        in_specs=[IN_SMEM, IN_VMEM] + [IN_HBM] * count + [ANYWHERE] * len(after),
        out_specs=[IN_VMEM] * 2,
        out_shape=[result] * 2,
        scratch_shapes=[pltpu.VMEM((slots, depth, sub), BF16), pltpu.SemaphoreType.DMA((slots,))],
        compiler_params=params(12 * MIB),
        cost_estimate=cost(1, 1),
    )(me, rows, *weights, *after)


def back_kernel(me_ref, rows_ref, weight_ref, *refs):
    outs, turned_ref = refs[-3:-1], refs[-1]
    quarter = outs[0].shape[2]
    sub = sub_width(quarter)
    turned_ref[...] = rows_ref[...].astype(F32).T.astype(BF16)
    for out_ref, offset in zip(outs, ((3, 1), (2, 0))):
        for k in range(2):
            base = (me_ref[0] ^ offset[k]) * quarter
            for c in range(0, quarter, sub):
                piece = weight_ref[pl.ds(pl.multiple_of(base + c, sub), sub), :]
                product = jnp.dot(piece, turned_ref[...], preferred_element_type=F32)
                out_ref[k, :, c : c + sub] = product.T.astype(BF16)


def back_products(me, rows, weight):
    height, depth = rows.shape
    quarter = weight.shape[0] // 4
    result = jax.ShapeDtypeStruct((2, height, quarter), BF16)
    return pl.pallas_call(
        back_kernel,
        in_specs=[IN_SMEM] + [IN_VMEM] * 2,
        out_specs=[IN_VMEM] * 2,
        out_shape=[result] * 2,
        scratch_shapes=[pltpu.VMEM((depth, height), BF16)],
        compiler_params=params(8 * MIB),
        cost_estimate=cost(1, 1),
    )(me, rows, weight)


def down_kernel(offsets, has_start, me_ref, first_ref, second_ref, weight_ref, *rest):
    out_ref = rest[-1]
    quarter = first_ref.shape[1]
    width = weight_ref.shape[1]
    sub = sub_width(width)
    for c in range(0, width, sub):
        total = rest[0][:, c : c + sub] if has_start else 0.0
        for rows_ref, offset in zip((first_ref, second_ref), offsets):
            base = pl.multiple_of((me_ref[0] ^ offset) * quarter, quarter)
            piece = weight_ref[pl.ds(base, quarter), c : c + sub]
            total += jnp.dot(rows_ref[...], piece, preferred_element_type=F32)
        out_ref[:, c : c + sub] = total.astype(out_ref.dtype)


def down_products(me, first, second, weight, offsets, start, out_type):
    height, quarter = first.shape
    width = weight.shape[1]
    operands = [first, second, weight] + ([] if start is None else [start])
    return pl.pallas_call(
        functools.partial(down_kernel, offsets, start is not None),
        in_specs=[IN_SMEM] + [IN_VMEM] * len(operands),
        out_specs=IN_VMEM,
        out_shape=jax.ShapeDtypeStruct((height, width), out_type),
        compiler_params=params(4 * MIB),
        cost_estimate=cost(1, 1),
    )(me, *operands)


def outer_kernel(offsets, counts, me_ref, tokens_ref, *refs):
    terms = refs[: len(offsets)]
    outs, (slots_ref, sems) = refs[-2 - counts : -2], refs[-2:]
    quarter = terms[0].shape[2]
    sub = slots_ref.shape[2]
    copies = []
    for term_ref, offset in zip(terms, offsets):
        base = (me_ref[0] ^ offset) * quarter
        for k in range(counts):
            for c in range(0, quarter, sub):
                slot = len(copies) % SLOTS
                if len(copies) >= SLOTS:
                    copies[-SLOTS].wait()
                slots_ref[slot] = jnp.dot(
                    tokens_ref[...], term_ref[k, :, c : c + sub], preferred_element_type=F32
                ).astype(BF16)
                columns = pl.ds(pl.multiple_of(base + c, sub), sub)
                copy = pltpu.make_async_copy(
                    slots_ref.at[slot], outs[k].at[:, columns], sems.at[slot]
                )
                copy.start()
                copies.append(copy)
    for copy in copies[-SLOTS:]:
        copy.wait()


def outer_products(me, tokens, terms, offsets, outputs):
    width, height = tokens.shape
    counts, unused, quarter = terms[0].shape
    sub = sub_width(quarter)
    given = [] if outputs is None else list(outputs)
    operands = [tokens, *terms]
    whole = jax.ShapeDtypeStruct((width, 4 * quarter), BF16)
    return pl.pallas_call(
        functools.partial(outer_kernel, offsets, counts),
        in_specs=[IN_SMEM] + [IN_VMEM] * len(operands) + [ANYWHERE] * len(given),
        out_specs=[ANYWHERE] * counts,
        out_shape=[whole] * counts,
        input_output_aliases={1 + len(operands) + k: k for k in range(len(given))},
        scratch_shapes=[
            pltpu.VMEM((SLOTS, width, sub), BF16),
            pltpu.SemaphoreType.DMA((SLOTS,)),
        ],
        compiler_params=params(14 * MIB),
        cost_estimate=cost(
            2 * counts * len(terms) * height * width * quarter,
            2 * counts * len(terms) * width * quarter,
        ),
    )(me, *operands, *given)


def turn_kernel(rows_ref, out_ref):
    out_ref[...] = rows_ref[...].astype(F32).T.astype(BF16)


def turn(rows):
    return pl.pallas_call(
        turn_kernel,
        in_specs=[IN_VMEM],
        out_specs=IN_VMEM,
        out_shape=jax.ShapeDtypeStruct(rows.shape[::-1], rows.dtype),
        cost_estimate=cost(1, 1),
    )(rows)


def fence_kernel(value_ref, *refs):
    refs[-1][...] = value_ref[...]


def fence(value, *after):
    return pl.pallas_call(
        fence_kernel,
        in_specs=[IN_VMEM] + [ANYWHERE] * len(after),
        out_specs=IN_VMEM,
        out_shape=jax.ShapeDtypeStruct(value.shape, value.dtype),
        cost_estimate=cost(1, 1),
    )(value, *after)


def near_sum(keep, got):
    return keep.astype(F32) + got.astype(F32)


def exchange(pieces):
    ranks = lax.axis_size("expert")
    if ranks <= 4:
        return [pieces[0]] + [swap(pieces[i], "expert", i) for i in range(1, ranks)]
    order = lax.axis_index("expert") ^ jnp.arange(ranks)
    stacked = jnp.take(jnp.stack(pieces), order, axis=0)
    moved = lax.all_to_all(stacked, "expert", split_axis=0, concat_axis=0, tiled=True)
    moved = jnp.take(moved, order, axis=0)
    return [moved[i] for i in range(ranks)]


def routing_tables(expert_ids, route_weights, expert_list, capacity):
    matches = expert_ids[None, :, :] == expert_list[:, None, None]
    chosen = jnp.any(matches, axis=2)
    route_share = jnp.sum(jnp.where(matches, route_weights[None, :, :], F32(0.0)), axis=2)
    place = jnp.cumsum(chosen.astype(jnp.int32), axis=1) - 1
    slot_ids = jnp.arange(capacity, dtype=jnp.int32)
    route_table = chosen[:, None, :] & (place[:, None, :] == slot_ids[None, :, None])
    return route_table, route_share


def per_device(
    tokens, expert_ids, route_weights, gate_weight, up_weight, down_weight, gate_probe, up_probe
):
    tok_rows, width_dev = tokens.shape
    capacity = tok_rows // 2
    ranks = lax.axis_size("expert")
    per_expert = ranks // EXPERTS
    token_total = ranks * tok_rows
    me = lax.axis_index("dp").astype(jnp.int32).reshape(1)
    mine = lax.axis_index("expert") // per_expert
    expert_list = jnp.stack([mine, 1 - mine]).astype(expert_ids.dtype)

    route_table, route_share = routing_tables(expert_ids, route_weights, expert_list, capacity)
    spread = route_table.astype(F32) * route_share[:, None, :]
    slots = jnp.einsum(
        "ect,tf->ecf", route_table.astype(BF16), tokens, preferred_element_type=F32
    ).astype(BF16)
    slot_rows = jnp.concatenate(exchange([slots[i // per_expert] for i in range(ranks)]), axis=0)

    def far_half(weight, after):
        send, keep = quarter_products(me, slot_rows, [weight], (3, 2), after)
        far = near_sum(keep[0], swap(send, "dp", 1)[0]).astype(BF16)
        return far, swap(far, "dp", 2)

    def near_half(weights, after):
        send, keep = quarter_products(me, slot_rows, weights, (1, 0), after)
        half = send.shape[1] // 2
        got = [swap(send[:, :half], "dp", 1), swap(send[:, half:], "dp", 1)]
        return near_sum(keep, jnp.concatenate(got, axis=1))

    far_gate, gate_across = far_half(gate_weight, ())
    far_up, up_across = far_half(up_weight, ())
    far_gate_tangent, gate_tangent_across = far_half(gate_probe, [far_gate])
    far_up_tangent, up_tangent_across = far_half(up_probe, [far_up])
    near = near_half([gate_weight, up_weight], [far_gate_tangent, gate_across])
    near_tangent = near_half([gate_probe, up_probe], [far_up_tangent, up_across])
    gate_value = near[0] + gate_across.astype(F32)
    up_value = near[1] + up_across.astype(F32)
    gate_tangent = near_tangent[0] + gate_tangent_across.astype(F32)
    up_tangent = near_tangent[1] + up_tangent_across.astype(F32)

    s = jax.nn.sigmoid(gate_value)
    active = gate_value * s
    slope = s + gate_value * s * (1.0 - s)
    bend = s * (1.0 - s) * (2.0 + gate_value * (1.0 - 2.0 * s))

    def through_down(own):
        beside = swap(own, "dp", 1)
        across = swap(own, "dp", 2)
        half = down_products(me, own, beside, down_weight, (0, 1), None, F32)
        return down_products(
            me, across, swap(across, "dp", 1), down_weight, (2, 3), half, BF16
        )

    def back(rows):
        send, keep = back_products(me, rows, down_weight)
        got = swap(send, "dp", 1)
        far = near_sum(keep[0], got[0]).astype(BF16)
        return near_sum(keep[1], got[1]) + swap(far, "dp", 2).astype(F32)

    def mix(out):
        came = exchange(list(out.reshape(ranks, capacity, width_dev)))
        sums = jnp.stack(
            [
                sum(piece.astype(F32) for piece in came[e * per_expert : (e + 1) * per_expert])
                for e in range(EXPERTS)
            ]
        )
        mixed = jnp.einsum("ect,ecf->tf", spread, sums, precision=lax.Precision.HIGHEST)
        cot = jnp.einsum(
            "ect,tf->ecf", spread, mixed / token_total, precision=lax.Precision.HIGHEST
        ).astype(BF16)
        return jnp.concatenate(exchange([cot[i // per_expert] for i in range(ranks)]), axis=0)

    hidden = (active * up_value).astype(BF16)
    cot_rows = mix(through_down(hidden))
    back_value = back(cot_rows)

    hidden_tangent = (slope * gate_tangent * up_value + active * up_tangent).astype(BF16)
    cot_tangent_rows = mix(through_down(hidden_tangent))
    back_tangent = back(cot_tangent_rows)

    gate_term = (
        back_tangent * up_value * slope
        + back_value * up_tangent * slope
        + back_value * up_value * bend * gate_tangent
    ).astype(BF16)
    up_term = (back_tangent * active + back_value * slope * gate_tangent).astype(BF16)

    turned = turn(slot_rows)
    terms = jnp.stack([gate_term, up_term])
    across = swap(terms, "dp", 2)
    outputs = outer_products(me, turned, [terms, swap(terms, "dp", 1)], (0, 1), None)
    across = fence(across, *outputs)
    beyond = swap(across, "dp", 1)
    outputs = outer_products(me, turned, [across], (2,), outputs)
    outputs = outer_products(me, turned, [beyond], (3,), outputs)
    return tuple(outputs)


def solution(mesh):
    return jax.shard_map(
        per_device,
        mesh=mesh,
        in_specs=(
            P(("groups", "expert"), "dp"),
            P(("groups", "expert"), None),
            P(("groups", "expert"), None),
            P("dp", "expert"),
            P("dp", "expert"),
            P("expert", "dp"),
            P("dp", "expert"),
            P("dp", "expert"),
        ),
        out_specs=(P(("groups", "dp"), "expert"), P(("groups", "dp"), "expert")),
        check_vma=False,
    )
```

```python
import functools

import jax
import jax.numpy as jnp
from jax import lax
from jax.experimental import pallas as pl
from jax.experimental.pallas import tpu as pltpu
from jax.sharding import PartitionSpec as P

EXPERTS = 2
BF16 = jnp.bfloat16
F32 = jnp.float32
KIB = 1024
MIB = 1024 * KIB
IN_VMEM = pl.BlockSpec(memory_space=pltpu.VMEM)
IN_SMEM = pl.BlockSpec(memory_space=pltpu.SMEM)
IN_HBM = pl.BlockSpec(memory_space=pltpu.HBM)
ANYWHERE = pl.BlockSpec(memory_space=pl.ANY)
PARTS = 2
ROWS = 16


def swap(value, axis, mask):
    size = lax.axis_size(axis)
    return lax.ppermute(value, axis, [(i, i ^ mask) for i in range(size)])


def sub_width(width):
    return 512 if width % 512 == 0 else width


def params(limit):
    return pltpu.CompilerParams(vmem_limit_bytes=limit)


def cost(flops, size):
    return pl.CostEstimate(flops=flops, bytes_accessed=size, transcendentals=0)


def prefetch_kernel(offsets, me_ref, *refs):
    weights, halves, sems = refs[: (len(refs) - 1) // 2], refs[(len(refs) - 1) // 2 : -1], refs[-1]
    quarter = halves[0].shape[2]
    copies = []
    for k, (weight_ref, half_ref) in enumerate(zip(weights, halves)):
        for p, offset in enumerate(offsets):
            base = pl.multiple_of((me_ref[0] ^ offset) * quarter, quarter)
            copies.append(
                pltpu.make_async_copy(
                    weight_ref.at[:, pl.ds(base, quarter)], half_ref.at[p], sems.at[k, p]
                )
            )
    for copy in copies:
        copy.start()
    for copy in copies:
        copy.wait()


def prefetch(me, weights, offsets):
    count, (depth, width) = len(weights), weights[0].shape
    half = (len(offsets), depth, width // 4)
    return pl.pallas_call(
        functools.partial(prefetch_kernel, offsets),
        in_specs=[IN_SMEM] + [IN_HBM] * count,
        out_specs=[IN_VMEM] * count,
        out_shape=[pltpu.VMEM(half, BF16)] * count,
        scratch_shapes=[pltpu.SemaphoreType.DMA((count, len(offsets)))],
        compiler_params=params(36 * MIB),
        cost_estimate=cost(1, 2 * count * depth * width),
    )(me, *weights)


def put(parts, rows, value):
    for i, part in enumerate(parts):
        part[...] = value[i * rows : (i + 1) * rows].astype(BF16)


def resident_kernel(rows_ref, half_ref, *refs):
    sends, keep_ref = refs[-1 - PARTS : -1], refs[-1]
    quarter = keep_ref.shape[2]
    sub = sub_width(quarter)
    for p in range(2):
        for c in range(0, quarter, sub):
            product = jnp.dot(
                rows_ref[...], half_ref[p, :, c : c + sub], preferred_element_type=F32
            )
            if p == 0:
                put([ref.at[:, c : c + sub] for ref in sends], sends[0].shape[0], product)
            else:
                keep_ref[0, :, c : c + sub] = product.astype(BF16)


def result_shapes(count, height, quarter):
    part = jax.ShapeDtypeStruct((height // PARTS, quarter), BF16)
    return [part] * (PARTS * count) + [jax.ShapeDtypeStruct((count, height, quarter), BF16)]


def resident_products(rows, half, after):
    shapes = result_shapes(1, rows.shape[0], half.shape[2])
    *send, keep = pl.pallas_call(
        resident_kernel,
        in_specs=[IN_VMEM] * 2 + [ANYWHERE] * len(after),
        out_specs=[IN_VMEM] * len(shapes),
        out_shape=shapes,
        compiler_params=params(4 * MIB),
        cost_estimate=cost(1, 1),
    )(rows, half, *after)
    return send, keep


def stream_kernel(count, offsets, me_ref, rows_ref, *refs):
    weights, (keep_ref, slots_ref, sems) = refs[:count], refs[-3:]
    sends = refs[-3 - PARTS * count : -3]
    quarter = keep_ref.shape[2]
    slots, unused, sub = slots_ref.shape
    copies, targets = [], []
    for k in range(count):
        for p, offset in enumerate(offsets):
            base = (me_ref[0] ^ offset) * quarter
            for c in range(0, quarter, sub):
                columns = pl.ds(pl.multiple_of(base + c, sub), sub)
                slot = len(copies) % slots
                copies.append(
                    pltpu.make_async_copy(
                        weights[k].at[:, columns], slots_ref.at[slot], sems.at[slot]
                    )
                )
                targets.append((k, p, c))
    for copy in copies[:slots]:
        copy.start()
    for i, (k, p, c) in enumerate(targets):
        copies[i].wait()
        product = jnp.dot(rows_ref[...], slots_ref[i % slots], preferred_element_type=F32)
        if p == 0:
            parts = sends[PARTS * k : PARTS * (k + 1)]
            put([ref.at[:, c : c + sub] for ref in parts], parts[0].shape[0], product)
        else:
            keep_ref[k, :, c : c + sub] = product.astype(BF16)
        if i + slots < len(copies):
            copies[i + slots].start()


def stream_products(me, rows, weights, offsets, after):
    count, (height, depth) = len(weights), rows.shape
    quarter = weights[0].shape[1] // 4
    sub = sub_width(quarter)
    slots = min(4, 2 * count * (quarter // sub))
    shapes = result_shapes(count, height, quarter)
    *send, keep = pl.pallas_call(
        functools.partial(stream_kernel, count, offsets),
        in_specs=[IN_SMEM, IN_VMEM] + [IN_HBM] * count + [ANYWHERE] * len(after),
        out_specs=[IN_VMEM] * len(shapes),
        out_shape=shapes,
        scratch_shapes=[pltpu.VMEM((slots, depth, sub), BF16), pltpu.SemaphoreType.DMA((slots,))],
        compiler_params=params(48 * MIB),
        cost_estimate=cost(1, 1),
    )(me, rows, *weights, *after)
    return send, keep


def stacked(pieces):
    return jnp.concatenate([piece[...].astype(F32) for piece in pieces], axis=0)


def back_kernel(count, offsets, me_ref, *refs):
    pieces, weight_ref = refs[:count], refs[count]
    sends, (keep_ref, turned_ref) = refs[-2 - 2 * PARTS : -2], refs[-2:]
    unused, height, quarter = keep_ref.shape
    sub = sub_width(quarter)
    turned_ref[...] = stacked(pieces).T.astype(BF16)
    for p, offset in enumerate(offsets):
        base = (me_ref[0] ^ offset) * quarter
        for c in range(0, quarter, sub):
            piece = weight_ref[pl.ds(pl.multiple_of(base + c, sub), sub), :]
            product = jnp.dot(piece, turned_ref[...], preferred_element_type=F32).T
            if p == 0:
                put([ref.at[:, c : c + sub] for ref in sends], sends[0].shape[0], product)
            else:
                keep_ref[0, :, c : c + sub] = product[:height].astype(BF16)
                keep_ref[1, :, c : c + sub] = product[height:].astype(BF16)


def back_products(me, pieces, weight, offsets, after):
    count, (rows, depth) = len(pieces), pieces[0].shape
    height, quarter = count * rows // 2, weight.shape[0] // 4
    shapes = result_shapes(2, height, quarter)
    *send, keep = pl.pallas_call(
        functools.partial(back_kernel, count, offsets),
        in_specs=[IN_SMEM] + [IN_VMEM] * (count + 1) + [ANYWHERE] * len(after),
        out_specs=[IN_VMEM] * len(shapes),
        out_shape=shapes,
        scratch_shapes=[pltpu.VMEM((depth, 2 * height), BF16)],
        compiler_params=params(8 * MIB),
        cost_estimate=cost(1, 1),
    )(me, *pieces, weight, *after)
    return send, keep


def down_kernel(offsets, has_start, pieces, me_ref, first_ref, second_ref, weight_ref, *rest):
    outs = rest[-pieces:]
    quarter = first_ref.shape[1]
    width = weight_ref.shape[1]
    sub = sub_width(width)
    for c in range(0, width, sub):
        total = rest[0][:, c : c + sub] if has_start else 0.0
        for rows_ref, offset in zip((first_ref, second_ref), offsets):
            base = pl.multiple_of((me_ref[0] ^ offset) * quarter, quarter)
            piece = weight_ref[pl.ds(base, quarter), c : c + sub]
            total += jnp.dot(rows_ref[...], piece, preferred_element_type=F32)
        for i, out_ref in enumerate(outs):
            rows = out_ref.shape[0]
            out_ref[:, c : c + sub] = total[i * rows : (i + 1) * rows].astype(out_ref.dtype)


def down_products(me, first, second, weight, offsets, start, pieces, out_type, after=()):
    height, quarter = first.shape
    width = weight.shape[1]
    operands = [first, second, weight] + ([] if start is None else [start])
    return pl.pallas_call(
        functools.partial(down_kernel, offsets, start is not None, pieces),
        in_specs=[IN_SMEM] + [IN_VMEM] * len(operands) + [ANYWHERE] * len(after),
        out_specs=[IN_VMEM] * pieces,
        out_shape=[jax.ShapeDtypeStruct((height // pieces, width), out_type)] * pieces,
        compiler_params=params(4 * MIB),
        cost_estimate=cost(1, 1),
    )(me, *operands, *after)


def mix_kernel(count, token_total, *refs):
    pieces, spread_ref, outs = refs[:count], refs[count], refs[-EXPERTS:]
    per_expert = count // EXPERTS
    mixed = 0.0
    for e in range(EXPERTS):
        total = 0.0
        for piece in pieces[e * per_expert : (e + 1) * per_expert]:
            total += piece[...].astype(F32)
        mixed += lax.dot_general(
            spread_ref[e],
            total,
            (((0,), (0,)), ((), ())),
            precision=lax.Precision.HIGHEST,
            preferred_element_type=F32,
        )
    mixed = mixed / token_total
    for e in range(EXPERTS):
        outs[e][...] = jnp.dot(
            spread_ref[e], mixed, precision=lax.Precision.HIGHEST, preferred_element_type=F32
        ).astype(BF16)


def mix_products(pieces, spread, token_total, after=()):
    count = len(pieces)
    result = jax.ShapeDtypeStruct(pieces[0].shape, BF16)
    return pl.pallas_call(
        functools.partial(mix_kernel, count, token_total),
        in_specs=[IN_VMEM] * (count + 1) + [ANYWHERE] * len(after),
        out_specs=[IN_VMEM] * EXPERTS,
        out_shape=[result] * EXPERTS,
        compiler_params=params(8 * MIB),
        cost_estimate=cost(1, 1),
    )(*pieces, spread, *after)


def outer_kernel(offsets, me_ref, tokens_ref, *refs):
    terms, (turned_ref, slots_ref, sems) = refs[: len(offsets)], refs[-3:]
    outs = refs[-5:-3]
    if len(offsets) == 2:
        outs, flag_ref = refs[-6:-4], refs[-4]
        flag_ref[...] = jnp.zeros_like(flag_ref)
    quarter = terms[0].shape[2]
    slots, unused, sub = slots_ref.shape
    turned_ref[...] = tokens_ref[...].astype(F32).T.astype(BF16)
    copies = []
    for term_ref, offset in zip(terms, offsets):
        base = (me_ref[0] ^ offset) * quarter
        for k in range(2):
            for c in range(0, quarter, sub):
                slot = len(copies) % slots
                if len(copies) >= slots:
                    copies[-slots].wait()
                slots_ref[slot] = jnp.dot(
                    turned_ref[...], term_ref[k, :, c : c + sub], preferred_element_type=F32
                ).astype(BF16)
                columns = pl.ds(pl.multiple_of(base + c, sub), sub)
                copy = pltpu.make_async_copy(
                    slots_ref.at[slot], outs[k].at[:, columns], sems.at[slot]
                )
                copy.start()
                copies.append(copy)
    for copy in copies[-slots:]:
        copy.wait()


def outer_products(me, tokens, terms, offsets, outputs):
    height, width = tokens.shape
    quarter = terms[0].shape[2]
    sub = sub_width(quarter)
    slots = min(4, 2 * len(terms) * (quarter // sub))
    operands = [tokens, *terms]
    given = [] if outputs is None else list(outputs)
    flags = len(offsets) - 1
    return pl.pallas_call(
        functools.partial(outer_kernel, offsets),
        in_specs=[IN_SMEM] + [IN_VMEM] * len(operands) + [ANYWHERE] * len(given),
        out_specs=[ANYWHERE] * 2 + [IN_VMEM] * flags,
        out_shape=[jax.ShapeDtypeStruct((width, 4 * quarter), BF16)] * 2
        + [jax.ShapeDtypeStruct((8, 128), F32)] * flags,
        input_output_aliases={1 + len(operands) + k: k for k in range(len(given))},
        scratch_shapes=[
            pltpu.VMEM((width, height), BF16),
            pltpu.VMEM((slots, width, sub), BF16),
            pltpu.SemaphoreType.DMA((slots,)),
        ],
        compiler_params=params(14 * MIB),
        cost_estimate=cost(1, 1),
    )(me, *operands, *given)


def rows_kernel(function, count, results, *refs):
    ins, outs = refs[:count], refs[-results:]
    height = outs[0].shape[-2]
    for low in range(0, height, ROWS):

        def load(i):
            ref = ins[i]
            if ref.shape[-2] == height:
                return ref[..., low : low + ROWS, :].astype(F32)
            part, start = divmod(low, ref.shape[-2])
            return ins[i + part][start : start + ROWS].astype(F32)

        for ref, value in zip(outs, function(load)):
            ref[..., low : low + ROWS, :] = value.astype(ref.dtype)


def by_rows(function, operands, shapes, after):
    return pl.pallas_call(
        functools.partial(rows_kernel, function, len(operands), len(shapes)),
        in_specs=[IN_VMEM] * len(operands) + [ANYWHERE] * len(after),
        out_specs=[IN_VMEM] * len(shapes),
        out_shape=[jax.ShapeDtypeStruct(shape, dtype) for shape, dtype in shapes],
        compiler_params=params(12 * MIB),
        cost_estimate=cost(1, 1),
    )(*operands, *after)


def far_rows(load):
    return (load(0)[0] + load(1),)


def far_pair_rows(load):
    near = load(0)
    return (jnp.stack([near[0] + load(1), near[1] + load(1 + PARTS)]),)


def hidden_rows(load):
    near = load(0)
    gate_value = near[0] + load(1) + load(1 + 2 * PARTS)
    up_value = near[1] + load(1 + PARTS) + load(2 + 2 * PARTS)
    return gate_value * jax.nn.sigmoid(gate_value) * up_value, gate_value, up_value


def tangent_rows(load):
    near = load(0)
    gate_tangent = near[0] + load(1) + load(1 + 2 * PARTS)
    up_tangent = near[1] + load(1 + PARTS) + load(2 + 2 * PARTS)
    gate_value, up_value = load(3 + 2 * PARTS), load(4 + 2 * PARTS)
    s = jax.nn.sigmoid(gate_value)
    slope = s + gate_value * s * (1.0 - s)
    hidden_tangent = slope * gate_tangent * up_value + gate_value * s * up_tangent
    return hidden_tangent, gate_tangent, up_tangent


def term_rows(load):
    near, across = load(0), load(1)
    back_value = near[0] + load(2) + across[0]
    back_tangent = near[1] + load(2 + PARTS) + across[1]
    gate_value, up_value, gate_tangent, up_tangent = (load(2 + 2 * PARTS + i) for i in range(4))
    s = jax.nn.sigmoid(gate_value)
    slope = s + gate_value * s * (1.0 - s)
    bend = s * (1.0 - s) * (2.0 + gate_value * (1.0 - 2.0 * s))
    gate_term = (
        back_tangent * up_value * slope
        + back_value * up_tangent * slope
        + back_value * up_value * bend * gate_tangent
    )
    up_term = back_tangent * (gate_value * s) + back_value * slope * gate_tangent
    return (jnp.stack([gate_term, up_term]),)


def pass_kernel(value_ref, *refs):
    refs[-1][...] = value_ref[...]


def pass_on(value, after):
    return pl.pallas_call(
        pass_kernel,
        in_specs=[IN_VMEM] + [ANYWHERE] * len(after),
        out_specs=IN_VMEM,
        out_shape=jax.ShapeDtypeStruct(value.shape, value.dtype),
        compiler_params=params(4 * MIB),
        cost_estimate=cost(1, 1),
    )(value, *after)


def exchange(pieces):
    ranks = lax.axis_size("expert")
    if ranks <= 4:
        return [pieces[0]] + [swap(pieces[i], "expert", i) for i in range(1, ranks)]
    order = lax.axis_index("expert") ^ jnp.arange(ranks)
    stacked = jnp.take(jnp.stack(pieces), order, axis=0)
    moved = lax.all_to_all(stacked, "expert", split_axis=0, concat_axis=0, tiled=True)
    moved = jnp.take(moved, order, axis=0)
    return [moved[i] for i in range(ranks)]


def routing_tables(expert_ids, route_weights, expert_list, capacity):
    matches = expert_ids[None, :, :] == expert_list[:, None, None]
    chosen = jnp.any(matches, axis=2)
    route_share = jnp.sum(jnp.where(matches, route_weights[None, :, :], F32(0.0)), axis=2)
    place = jnp.cumsum(chosen.astype(jnp.int32), axis=1) - 1
    slot_ids = jnp.arange(capacity, dtype=jnp.int32)
    route_table = chosen[:, None, :] & (place[:, None, :] == slot_ids[None, :, None])
    return route_table, route_share


def per_device(
    tokens, expert_ids, route_weights, gate_weight, up_weight, down_weight, gate_probe, up_probe
):
    tok_rows, width_dev = tokens.shape
    capacity = tok_rows // 2
    ranks = lax.axis_size("expert")
    per_expert = ranks // EXPERTS
    token_total = ranks * tok_rows
    me = lax.axis_index("dp").astype(jnp.int32).reshape(1)
    mine = lax.axis_index("expert") // per_expert
    expert_list = jnp.stack([mine, 1 - mine]).astype(expert_ids.dtype)

    route_table, route_share = routing_tables(expert_ids, route_weights, expert_list, capacity)
    spread = route_table.astype(F32) * route_share[:, None, :]
    slots = jnp.einsum(
        "ect,tf->ecf", route_table.astype(BF16), tokens, preferred_element_type=F32
    ).astype(BF16)
    slot_rows = jnp.concatenate(exchange([slots[i // per_expert] for i in range(ranks)]), axis=0)

    def core(parts):
        return [swap(part, "dp", 1) for part in parts]

    height, quarter = slot_rows.shape[0], down_weight.shape[0] // 4
    part_type = ((height, quarter), BF16)
    wide_type = ((height, quarter), F32)

    def far_sum(keep, got, after):
        (far,) = by_rows(far_rows, [keep, *got], [part_type], after)
        return far, swap(far, "dp", 2)

    halves = prefetch(me, [gate_weight, up_weight, gate_probe], (3, 2))
    send, keep = resident_products(slot_rows, halves[0], [])
    gate_far = (keep, core(send))
    send, keep = resident_products(slot_rows, halves[1], [keep])
    up_far = (keep, core(send))
    far, gate_across = far_sum(*gate_far, [keep])
    send, keep = resident_products(slot_rows, halves[2], [far])
    gate_tangent_far = (keep, core(send))
    far, up_across = far_sum(*up_far, [keep])
    send, near = stream_products(me, slot_rows, [gate_weight, up_weight], (1, 0), [far])
    near_got = core(send)
    far, gate_tangent_across = far_sum(*gate_tangent_far, [near])
    send, near_tangent = stream_products(
        me, slot_rows, [gate_probe, up_probe], (1, 0), [far, gate_across]
    )
    near_tangent_got = core(send)
    hidden, gate_value, up_value = by_rows(
        hidden_rows,
        [near, *near_got, gate_across, up_across],
        [part_type, wide_type, wide_type],
        [near_tangent, gate_tangent_across],
    )
    beside, across = swap(hidden, "dp", 1), swap(hidden, "dp", 2)
    send, keep = stream_products(
        me, slot_rows, [up_probe], (3, 2), [hidden]
    )
    got = core(send)
    (half,) = down_products(
        me, hidden, beside, down_weight, (0, 1), None, 1, F32, [keep]
    )
    far, up_tangent_across = far_sum(keep, got, [half])
    across = pass_on(across, [far])
    out = down_products(
        me, across, swap(across, "dp", 1), down_weight, (2, 3), half, ranks, BF16, [far]
    )
    came = exchange(out)

    hidden_tangent, gate_tangent, up_tangent = by_rows(
        tangent_rows,
        [
            near_tangent,
            *near_tangent_got,
            gate_tangent_across,
            up_tangent_across,
            gate_value,
            up_value,
        ],
        [part_type, wide_type, wide_type],
        [out[0], came[1]],
    )
    beside, across = swap(hidden_tangent, "dp", 1), swap(hidden_tangent, "dp", 2)
    (half,) = down_products(
        me, hidden_tangent, beside, down_weight, (0, 1), None, 1, F32, [hidden_tangent]
    )
    across = pass_on(across, [half])
    out = down_products(
        me, across, swap(across, "dp", 1), down_weight, (2, 3), half, ranks, BF16, []
    )
    came_tangent = exchange(out)
    cot = mix_products(came, spread, token_total, [out[0], came_tangent[1]])
    came = exchange([cot[i // per_expert] for i in range(ranks)])
    cot = mix_products(came_tangent, spread, token_total, [cot[0], came[1]])
    came += exchange([cot[i // per_expert] for i in range(ranks)])

    send, keep = back_products(me, came, down_weight, (3, 2), [])
    got = core(send)
    send, near = back_products(me, came, down_weight, (1, 0), [keep])
    pair_type = ((2, height, quarter), BF16)
    (far,) = by_rows(far_pair_rows, [keep, *got], [pair_type], [near])
    got = core(send)
    (terms,) = by_rows(
        term_rows,
        [near, swap(far, "dp", 2), *got, gate_value, up_value, gate_tangent, up_tangent],
        [pair_type],
        [far],
    )

    across, beside = swap(terms, "dp", 2), swap(terms, "dp", 1)
    *outputs, flag = outer_products(me, slot_rows, [terms, beside], (0, 1), None)
    across = pass_on(across, [flag])
    beyond = swap(across, "dp", 1)
    outputs = outer_products(me, slot_rows, [across], (2,), outputs)
    return tuple(outer_products(me, slot_rows, [beyond], (3,), outputs))


def solution(mesh):
    return jax.shard_map(
        per_device,
        mesh=mesh,
        in_specs=(
            P(("groups", "expert"), "dp"),
            P(("groups", "expert"), None),
            P(("groups", "expert"), None),
            P("dp", "expert"),
            P("dp", "expert"),
            P("expert", "dp"),
            P("dp", "expert"),
            P("dp", "expert"),
        ),
        out_specs=(P(("groups", "dp"), "expert"), P(("groups", "dp"), "expert")),
        check_vma=False,
    )
```

```python
import functools

import jax
import jax.numpy as jnp
from jax import lax
from jax.experimental import pallas as pl
from jax.experimental.pallas import tpu as pltpu
from jax.sharding import PartitionSpec as P

EXPERTS = 2
BF16 = jnp.bfloat16
F32 = jnp.float32
KIB = 1024
MIB = 1024 * KIB
IN_VMEM = pl.BlockSpec(memory_space=pltpu.VMEM)
IN_SMEM = pl.BlockSpec(memory_space=pltpu.SMEM)
IN_HBM = pl.BlockSpec(memory_space=pltpu.HBM)
ANYWHERE = pl.BlockSpec(memory_space=pl.ANY)
PARTS = 2
ROWS = 16


def swap(value, axis, mask):
    size = lax.axis_size(axis)
    return lax.ppermute(value, axis, [(i, i ^ mask) for i in range(size)])


def sub_width(width):
    return 512 if width % 512 == 0 else width


def params(limit):
    return pltpu.CompilerParams(vmem_limit_bytes=limit)


def cost(flops, size):
    return pl.CostEstimate(flops=flops, bytes_accessed=size, transcendentals=0)


def prefetch_kernel(offsets, me_ref, *refs):
    weights, halves, sems = refs[: (len(refs) - 1) // 2], refs[(len(refs) - 1) // 2 : -1], refs[-1]
    quarter = halves[0].shape[2]
    copies = []
    for k, (weight_ref, half_ref) in enumerate(zip(weights, halves)):
        for p, offset in enumerate(offsets):
            base = pl.multiple_of((me_ref[0] ^ offset) * quarter, quarter)
            copies.append(
                pltpu.make_async_copy(
                    weight_ref.at[:, pl.ds(base, quarter)], half_ref.at[p], sems.at[k, p]
                )
            )
    for copy in copies:
        copy.start()
    for copy in copies:
        copy.wait()


def prefetch(me, weights, offsets):
    count, (depth, width) = len(weights), weights[0].shape
    half = (len(offsets), depth, width // 4)
    return pl.pallas_call(
        functools.partial(prefetch_kernel, offsets),
        in_specs=[IN_SMEM] + [IN_HBM] * count,
        out_specs=[IN_VMEM] * count,
        out_shape=[pltpu.VMEM(half, BF16)] * count,
        scratch_shapes=[pltpu.SemaphoreType.DMA((count, len(offsets)))],
        compiler_params=params(36 * MIB),
        cost_estimate=cost(1, 2 * count * depth * width),
    )(me, *weights)


def put(parts, rows, value):
    for i, part in enumerate(parts):
        part[...] = value[i * rows : (i + 1) * rows].astype(BF16)


def resident_kernel(rows_ref, half_ref, *refs):
    sends, keep_ref = refs[-1 - PARTS : -1], refs[-1]
    quarter = keep_ref.shape[2]
    sub = sub_width(quarter)
    for p in range(2):
        for c in range(0, quarter, sub):
            product = jnp.dot(
                rows_ref[...], half_ref[p, :, c : c + sub], preferred_element_type=F32
            )
            if p == 0:
                put([ref.at[:, c : c + sub] for ref in sends], sends[0].shape[0], product)
            else:
                keep_ref[0, :, c : c + sub] = product.astype(BF16)


def result_shapes(count, height, quarter):
    part = jax.ShapeDtypeStruct((height // PARTS, quarter), BF16)
    return [part] * (PARTS * count) + [jax.ShapeDtypeStruct((count, height, quarter), BF16)]


def resident_products(rows, half, after):
    shapes = result_shapes(1, rows.shape[0], half.shape[2])
    *send, keep = pl.pallas_call(
        resident_kernel,
        in_specs=[IN_VMEM] * 2 + [ANYWHERE] * len(after),
        out_specs=[IN_VMEM] * len(shapes),
        out_shape=shapes,
        compiler_params=params(4 * MIB),
        cost_estimate=cost(1, 1),
    )(rows, half, *after)
    return send, keep


def stream_kernel(count, offsets, me_ref, rows_ref, *refs):
    weights, (keep_ref, slots_ref, sems) = refs[:count], refs[-3:]
    sends = refs[-3 - PARTS * count : -3]
    quarter = keep_ref.shape[2]
    slots, unused, sub = slots_ref.shape
    copies, targets = [], []
    for k in range(count):
        for p, offset in enumerate(offsets):
            base = (me_ref[0] ^ offset) * quarter
            for c in range(0, quarter, sub):
                columns = pl.ds(pl.multiple_of(base + c, sub), sub)
                slot = len(copies) % slots
                copies.append(
                    pltpu.make_async_copy(
                        weights[k].at[:, columns], slots_ref.at[slot], sems.at[slot]
                    )
                )
                targets.append((k, p, c))
    for copy in copies[:slots]:
        copy.start()
    for i, (k, p, c) in enumerate(targets):
        copies[i].wait()
        product = jnp.dot(rows_ref[...], slots_ref[i % slots], preferred_element_type=F32)
        if p == 0:
            parts = sends[PARTS * k : PARTS * (k + 1)]
            put([ref.at[:, c : c + sub] for ref in parts], parts[0].shape[0], product)
        else:
            keep_ref[k, :, c : c + sub] = product.astype(BF16)
        if i + slots < len(copies):
            copies[i + slots].start()


def stream_products(me, rows, weights, offsets, after):
    count, (height, depth) = len(weights), rows.shape
    quarter = weights[0].shape[1] // 4
    sub = sub_width(quarter)
    slots = min(4, 2 * count * (quarter // sub))
    shapes = result_shapes(count, height, quarter)
    *send, keep = pl.pallas_call(
        functools.partial(stream_kernel, count, offsets),
        in_specs=[IN_SMEM, IN_VMEM] + [IN_HBM] * count + [ANYWHERE] * len(after),
        out_specs=[IN_VMEM] * len(shapes),
        out_shape=shapes,
        scratch_shapes=[pltpu.VMEM((slots, depth, sub), BF16), pltpu.SemaphoreType.DMA((slots,))],
        compiler_params=params(48 * MIB),
        cost_estimate=cost(1, 1),
    )(me, rows, *weights, *after)
    return send, keep


def stacked(pieces):
    return jnp.concatenate([piece[...].astype(F32) for piece in pieces], axis=0)


def back_kernel(count, jobs, width, me_ref, *refs):
    pieces, weight_ref, turned_ref = refs[:count], refs[count], refs[-1]
    each = 3
    outs = refs[-1 - each * len(jobs) : -1]
    sub = sub_width(width)
    turned_ref[...] = stacked(pieces).T.astype(BF16)
    for job, (offsets, chunk, chunks) in enumerate(jobs):
        sends, keep_ref = outs[each * job : each * job + each - 1], outs[each * job + each - 1]
        height = keep_ref.shape[1]
        for p, offset in enumerate(offsets):
            base = (me_ref[0] ^ offset) * (width * chunks) + chunk * width
            for c in range(0, width, sub):
                piece = weight_ref[pl.ds(pl.multiple_of(base + c, sub), sub), :]
                product = jnp.dot(piece, turned_ref[...], preferred_element_type=F32).T
                if p == 0:
                    put([ref.at[:, c : c + sub] for ref in sends], height, product)
                else:
                    keep_ref[0, :, c : c + sub] = product[:height].astype(BF16)
                    keep_ref[1, :, c : c + sub] = product[height:].astype(BF16)


def back_products(me, pieces, weight, offsets, chunk_list, chunks, after):
    count, (rows, depth) = len(pieces), pieces[0].shape
    height, width = count * rows // 2, weight.shape[0] // (4 * chunks)
    part = jax.ShapeDtypeStruct((height, width), BF16)
    shapes = [part, part, jax.ShapeDtypeStruct((2, height, width), BF16)]
    each = len(shapes)
    jobs = [(offsets, chunk, chunks) for chunk in chunk_list]
    results = pl.pallas_call(
        functools.partial(back_kernel, count, jobs, width),
        in_specs=[IN_SMEM] + [IN_VMEM] * (count + 1) + [ANYWHERE] * len(after),
        out_specs=[IN_VMEM] * (each * len(jobs)),
        out_shape=shapes * len(jobs),
        scratch_shapes=[pltpu.VMEM((depth, 2 * height), BF16)],
        compiler_params=params(8 * MIB),
        cost_estimate=cost(1, 1),
    )(me, *pieces, weight, *after)
    return [
        (results[each * i : each * i + each - 1], results[each * i + each - 1])
        for i in range(len(jobs))
    ]


def down_kernel(offsets, has_start, pieces, me_ref, first_ref, second_ref, weight_ref, *rest):
    outs = rest[-pieces:]
    quarter = first_ref.shape[1]
    width = weight_ref.shape[1]
    sub = sub_width(width)
    for c in range(0, width, sub):
        total = rest[0][:, c : c + sub] if has_start else 0.0
        for rows_ref, offset in zip((first_ref, second_ref), offsets):
            base = pl.multiple_of((me_ref[0] ^ offset) * quarter, quarter)
            piece = weight_ref[pl.ds(base, quarter), c : c + sub]
            total += jnp.dot(rows_ref[...], piece, preferred_element_type=F32)
        for i, out_ref in enumerate(outs):
            rows = out_ref.shape[0]
            out_ref[:, c : c + sub] = total[i * rows : (i + 1) * rows].astype(out_ref.dtype)


def down_products(me, first, second, weight, offsets, start, pieces, out_type, after=()):
    height, quarter = first.shape
    width = weight.shape[1]
    operands = [first, second, weight] + ([] if start is None else [start])
    return pl.pallas_call(
        functools.partial(down_kernel, offsets, start is not None, pieces),
        in_specs=[IN_SMEM] + [IN_VMEM] * len(operands) + [ANYWHERE] * len(after),
        out_specs=[IN_VMEM] * pieces,
        out_shape=[jax.ShapeDtypeStruct((height // pieces, width), out_type)] * pieces,
        compiler_params=params(4 * MIB),
        cost_estimate=cost(1, 1),
    )(me, *operands, *after)


def mix_kernel(count, token_total, *refs):
    pieces, spread_ref, outs = refs[:count], refs[count], refs[-EXPERTS:]
    per_expert = count // EXPERTS
    mixed = 0.0
    for e in range(EXPERTS):
        total = 0.0
        for piece in pieces[e * per_expert : (e + 1) * per_expert]:
            total += piece[...].astype(F32)
        mixed += lax.dot_general(
            spread_ref[e],
            total,
            (((0,), (0,)), ((), ())),
            precision=lax.Precision.HIGHEST,
            preferred_element_type=F32,
        )
    mixed = mixed / token_total
    for e in range(EXPERTS):
        outs[e][...] = jnp.dot(
            spread_ref[e], mixed, precision=lax.Precision.HIGHEST, preferred_element_type=F32
        ).astype(BF16)


def mix_products(pieces, spread, token_total, after=()):
    count = len(pieces)
    result = jax.ShapeDtypeStruct(pieces[0].shape, BF16)
    return pl.pallas_call(
        functools.partial(mix_kernel, count, token_total),
        in_specs=[IN_VMEM] * (count + 1) + [ANYWHERE] * len(after),
        out_specs=[IN_VMEM] * EXPERTS,
        out_shape=[result] * EXPERTS,
        compiler_params=params(8 * MIB),
        cost_estimate=cost(1, 1),
    )(*pieces, spread, *after)


def outer_kernel(places, chunks, flags, me_ref, tokens_ref, *refs):
    terms = refs[: len(places)]
    outs, (turned_ref, slots_ref, sems) = refs[-5:-3], refs[-3:]
    if flags:
        outs = refs[-6:-4]
        refs[-4][...] = jnp.zeros_like(refs[-4])
    width = terms[0].shape[2]
    slots, unused, sub = slots_ref.shape
    turned_ref[...] = tokens_ref[...].astype(F32).T.astype(BF16)
    copies = []
    for term_ref, (offset, chunk) in zip(terms, places):
        base = (me_ref[0] ^ offset) * (width * chunks) + chunk * width
        for k in range(2):
            for c in range(0, width, sub):
                slot = len(copies) % slots
                if len(copies) >= slots:
                    copies[-slots].wait()
                slots_ref[slot] = jnp.dot(
                    turned_ref[...], term_ref[k, :, c : c + sub], preferred_element_type=F32
                ).astype(BF16)
                columns = pl.ds(pl.multiple_of(base + c, sub), sub)
                copy = pltpu.make_async_copy(
                    slots_ref.at[slot], outs[k].at[:, columns], sems.at[slot]
                )
                copy.start()
                copies.append(copy)
    for copy in copies[-slots:]:
        copy.wait()


def outer_products(me, tokens, terms, places, chunks, outputs, after=()):
    height, width = tokens.shape
    columns = terms[0].shape[2]
    sub = sub_width(columns)
    slots = min(4, 2 * len(terms) * (columns // sub))
    operands = [tokens, *terms]
    given = [] if outputs is None else list(outputs)
    flags = int(outputs is None)
    return pl.pallas_call(
        functools.partial(outer_kernel, places, chunks, flags),
        in_specs=[IN_SMEM]
        + [IN_VMEM] * len(operands)
        + [ANYWHERE] * (len(given) + len(after)),
        out_specs=[ANYWHERE] * 2 + [IN_VMEM] * flags,
        out_shape=[jax.ShapeDtypeStruct((width, 4 * chunks * columns), BF16)] * 2
        + [jax.ShapeDtypeStruct((8, 128), F32)] * flags,
        input_output_aliases={1 + len(operands) + k: k for k in range(len(given))},
        scratch_shapes=[
            pltpu.VMEM((width, height), BF16),
            pltpu.VMEM((slots, width, sub), BF16),
            pltpu.SemaphoreType.DMA((slots,)),
        ],
        compiler_params=params(14 * MIB),
        cost_estimate=cost(1, 1),
    )(me, *operands, *given, *after)


def rows_kernel(function, count, results, start_column, *refs):
    ins, outs = refs[:count], refs[-results:]
    height, width = outs[0].shape[-2:]
    for low in range(0, height, ROWS):

        def load(i):
            ref = ins[i]
            if ref.shape[-1] > width:
                return ref[low : low + ROWS, start_column : start_column + width].astype(F32)
            if ref.shape[-2] == height:
                return ref[..., low : low + ROWS, :].astype(F32)
            part, start = divmod(low, ref.shape[-2])
            return ins[i + part][start : start + ROWS].astype(F32)

        for ref, value in zip(outs, function(load)):
            ref[..., low : low + ROWS, :] = value.astype(ref.dtype)


def by_rows(function, operands, shapes, after, start_column=0):
    return pl.pallas_call(
        functools.partial(rows_kernel, function, len(operands), len(shapes), start_column),
        in_specs=[IN_VMEM] * len(operands) + [ANYWHERE] * len(after),
        out_specs=[IN_VMEM] * len(shapes),
        out_shape=[jax.ShapeDtypeStruct(shape, dtype) for shape, dtype in shapes],
        compiler_params=params(12 * MIB),
        cost_estimate=cost(1, 1),
    )(*operands, *after)


def far_rows(load):
    return (load(0)[0] + load(1),)


def far_pair_rows(load):
    near = load(0)
    return (jnp.stack([near[0] + load(1), near[1] + load(2)]),)


def hidden_rows(load):
    near = load(0)
    gate_value = near[0] + load(1) + load(1 + 2 * PARTS)
    up_value = near[1] + load(1 + PARTS) + load(2 + 2 * PARTS)
    return gate_value * jax.nn.sigmoid(gate_value) * up_value, gate_value, up_value


def tangent_rows(load):
    near = load(0)
    gate_tangent = near[0] + load(1) + load(1 + 2 * PARTS)
    up_tangent = near[1] + load(1 + PARTS) + load(2 + 2 * PARTS)
    gate_value, up_value = load(3 + 2 * PARTS), load(4 + 2 * PARTS)
    s = jax.nn.sigmoid(gate_value)
    slope = s + gate_value * s * (1.0 - s)
    hidden_tangent = slope * gate_tangent * up_value + gate_value * s * up_tangent
    return hidden_tangent, gate_tangent, up_tangent


def term_rows(load):
    near, across = load(0), load(1)
    back_value = near[0] + load(2) + across[0]
    back_tangent = near[1] + load(3) + across[1]
    gate_value, up_value, gate_tangent, up_tangent = (load(4 + i) for i in range(4))
    s = jax.nn.sigmoid(gate_value)
    slope = s + gate_value * s * (1.0 - s)
    bend = s * (1.0 - s) * (2.0 + gate_value * (1.0 - 2.0 * s))
    gate_term = (
        back_tangent * up_value * slope
        + back_value * up_tangent * slope
        + back_value * up_value * bend * gate_tangent
    )
    up_term = back_tangent * (gate_value * s) + back_value * slope * gate_tangent
    return (jnp.stack([gate_term, up_term]),)


def pass_kernel(value_ref, *refs):
    refs[-1][...] = value_ref[...]


def pass_on(value, after):
    return pl.pallas_call(
        pass_kernel,
        in_specs=[IN_VMEM] + [ANYWHERE] * len(after),
        out_specs=IN_VMEM,
        out_shape=jax.ShapeDtypeStruct(value.shape, value.dtype),
        compiler_params=params(4 * MIB),
        cost_estimate=cost(1, 1),
    )(value, *after)


def exchange(pieces):
    ranks = lax.axis_size("expert")
    if ranks <= 4:
        return [pieces[0]] + [swap(pieces[i], "expert", i) for i in range(1, ranks)]
    order = lax.axis_index("expert") ^ jnp.arange(ranks)
    stacked = jnp.take(jnp.stack(pieces), order, axis=0)
    moved = lax.all_to_all(stacked, "expert", split_axis=0, concat_axis=0, tiled=True)
    moved = jnp.take(moved, order, axis=0)
    return [moved[i] for i in range(ranks)]


def routing_tables(expert_ids, route_weights, expert_list, capacity):
    matches = expert_ids[None, :, :] == expert_list[:, None, None]
    chosen = jnp.any(matches, axis=2)
    route_share = jnp.sum(jnp.where(matches, route_weights[None, :, :], F32(0.0)), axis=2)
    place = jnp.cumsum(chosen.astype(jnp.int32), axis=1) - 1
    slot_ids = jnp.arange(capacity, dtype=jnp.int32)
    route_table = chosen[:, None, :] & (place[:, None, :] == slot_ids[None, :, None])
    return route_table, route_share


def per_device(
    tokens, expert_ids, route_weights, gate_weight, up_weight, down_weight, gate_probe, up_probe
):
    tok_rows, width_dev = tokens.shape
    capacity = tok_rows // 2
    ranks = lax.axis_size("expert")
    per_expert = ranks // EXPERTS
    token_total = ranks * tok_rows
    me = lax.axis_index("dp").astype(jnp.int32).reshape(1)
    mine = lax.axis_index("expert") // per_expert
    expert_list = jnp.stack([mine, 1 - mine]).astype(expert_ids.dtype)

    route_table, route_share = routing_tables(expert_ids, route_weights, expert_list, capacity)
    spread = route_table.astype(F32) * route_share[:, None, :]
    slots = jnp.einsum(
        "ect,tf->ecf", route_table.astype(BF16), tokens, preferred_element_type=F32
    ).astype(BF16)
    slot_rows = jnp.concatenate(exchange([slots[i // per_expert] for i in range(ranks)]), axis=0)

    def core(parts):
        return [swap(part, "dp", 1) for part in parts]

    height, quarter = slot_rows.shape[0], down_weight.shape[0] // 4
    part_type = ((height, quarter), BF16)
    wide_type = ((height, quarter), F32)

    def far_sum(keep, got, after):
        (far,) = by_rows(far_rows, [keep, *got], [part_type], after)
        return far, swap(far, "dp", 2)

    halves = prefetch(me, [gate_weight, up_weight, gate_probe], (3, 2))
    send, keep = resident_products(slot_rows, halves[0], [])
    gate_far = (keep, core(send))
    send, keep = resident_products(slot_rows, halves[1], [keep])
    up_far = (keep, core(send))
    far, gate_across = far_sum(*gate_far, [keep])
    send, keep = resident_products(slot_rows, halves[2], [far])
    gate_tangent_far = (keep, core(send))
    far, up_across = far_sum(*up_far, [keep])
    send, near = stream_products(me, slot_rows, [gate_weight, up_weight], (1, 0), [far])
    near_got = core(send)
    far, gate_tangent_across = far_sum(*gate_tangent_far, [near, gate_across, up_across])
    hidden, gate_value, up_value = by_rows(
        hidden_rows,
        [near, *near_got, gate_across, up_across],
        [part_type, wide_type, wide_type],
        [far],
    )
    beside, across = swap(hidden, "dp", 1), swap(hidden, "dp", 2)
    send, keep = stream_products(me, slot_rows, [up_probe], (3, 2), [hidden])
    got = core(send)
    (half_value,) = down_products(
        me, hidden, beside, down_weight, (0, 1), None, 1, F32, [keep]
    )
    far, up_tangent_across = far_sum(keep, got, [half_value])
    send, near_tangent = stream_products(
        me, slot_rows, [gate_probe, up_probe], (1, 0), [far, gate_tangent_across]
    )
    got = core(send)
    hidden_tangent, gate_tangent, up_tangent = by_rows(
        tangent_rows,
        [
            near_tangent,
            *got,
            gate_tangent_across,
            up_tangent_across,
            gate_value,
            up_value,
        ],
        [part_type, wide_type, wide_type],
        [],
    )
    out = down_products(
        me,
        across,
        swap(across, "dp", 1),
        down_weight,
        (2, 3),
        half_value,
        ranks,
        BF16,
        [hidden_tangent],
    )
    came = exchange(out)

    beside, across = swap(hidden_tangent, "dp", 1), swap(hidden_tangent, "dp", 2)
    (half,) = down_products(
        me, hidden_tangent, beside, down_weight, (0, 1), None, 1, F32, [out[0]]
    )
    across = pass_on(across, [half, came[1]])
    out = down_products(
        me, across, swap(across, "dp", 1), down_weight, (2, 3), half, ranks, BF16, []
    )
    came_tangent = exchange(out)
    cot = mix_products(came, spread, token_total, [out[0], came_tangent[1]])
    came = exchange([cot[i // per_expert] for i in range(ranks)])
    cot = mix_products(came_tangent, spread, token_total, [cot[0], came[1]])
    came += exchange([cot[i // per_expert] for i in range(ranks)])

    chunks = 2 if quarter % 256 == 0 else 1
    width = quarter // chunks
    pair_type = ((2, height, width), BF16)
    keep, ends = cot[0], []
    for i in range(chunks):
        ((send, keep),) = back_products(me, came, down_weight, (3, 2), [i], chunks, [keep])
        ends.append((keep, core(send)))
    fars = []
    for i in range(chunks - 1):
        fars += by_rows(far_pair_rows, [ends[i][0], *ends[i][1]], [pair_type], [keep])
    nears = back_products(me, came, down_weight, (1, 0), range(chunks), chunks, fars + [keep])
    fars += by_rows(far_pair_rows, [ends[-1][0], *ends[-1][1]], [pair_type], [nears[0][1]])
    sums = [swap(far, "dp", 2) for far in fars]
    nears = [[keep, *core(send)] for send, keep in nears]

    last, terms = fars[-1], []
    for i in range(chunks):
        (near, *got) = nears[i]
        terms += by_rows(
            term_rows,
            [near, sums[i], *got, gate_value, up_value, gate_tangent, up_tangent],
            [pair_type],
            [last],
            i * width,
        )
        last = terms[-1]
    across = [swap(term, "dp", 2) for term in terms]
    beside = [swap(term, "dp", 1) for term in terms]
    places = [(offset, i) for offset in (0, 1) for i in range(chunks)]
    *outputs, last = outer_products(me, slot_rows, terms + beside, places, chunks, None)
    passed = []
    for i in range(chunks):
        last = pass_on(across[i], [last])
        passed.append((last, swap(last, "dp", 1)))
    for i in range(chunks):
        outputs = outer_products(
            me, slot_rows, passed[i], [(2, i), (3, i)], chunks, outputs, [last]
        )
    return tuple(outputs)


def solution(mesh):
    return jax.shard_map(
        per_device,
        mesh=mesh,
        in_specs=(
            P(("groups", "expert"), "dp"),
            P(("groups", "expert"), None),
            P(("groups", "expert"), None),
            P("dp", "expert"),
            P("dp", "expert"),
            P("expert", "dp"),
            P("dp", "expert"),
            P("dp", "expert"),
        ),
        out_specs=(P(("groups", "dp"), "expert"), P(("groups", "dp"), "expert")),
        check_vma=False,
    )
```

```python
import functools

import jax
import jax.numpy as jnp
from jax import lax
from jax.experimental import pallas as pl
from jax.experimental.pallas import tpu as pltpu
from jax.sharding import PartitionSpec as P

EXPERTS = 2
BF16 = jnp.bfloat16
F32 = jnp.float32
KIB = 1024
MIB = 1024 * KIB
IN_VMEM = pl.BlockSpec(memory_space=pltpu.VMEM)
IN_SMEM = pl.BlockSpec(memory_space=pltpu.SMEM)
IN_HBM = pl.BlockSpec(memory_space=pltpu.HBM)
ANYWHERE = pl.BlockSpec(memory_space=pl.ANY)
PARTS = 2
ROWS = 16


def swap(value, axis, mask):
    size = lax.axis_size(axis)
    return lax.ppermute(value, axis, [(i, i ^ mask) for i in range(size)])


def sub_width(width):
    return 512 if width % 512 == 0 else width


def params(limit):
    return pltpu.CompilerParams(vmem_limit_bytes=limit)


def cost(flops, size):
    return pl.CostEstimate(flops=flops, bytes_accessed=size, transcendentals=0)


def prefetch_kernel(offsets, me_ref, *refs):
    weights, halves, sems = refs[: (len(refs) - 1) // 2], refs[(len(refs) - 1) // 2 : -1], refs[-1]
    quarter = halves[0].shape[2]
    copies = []
    for k, (weight_ref, half_ref) in enumerate(zip(weights, halves)):
        for p, offset in enumerate(offsets):
            base = pl.multiple_of((me_ref[0] ^ offset) * quarter, quarter)
            copies.append(
                pltpu.make_async_copy(
                    weight_ref.at[:, pl.ds(base, quarter)], half_ref.at[p], sems.at[k, p]
                )
            )
    for copy in copies:
        copy.start()
    for copy in copies:
        copy.wait()


def prefetch(me, weights, offsets):
    count, (depth, width) = len(weights), weights[0].shape
    half = (len(offsets), depth, width // 4)
    return pl.pallas_call(
        functools.partial(prefetch_kernel, offsets),
        in_specs=[IN_SMEM] + [IN_HBM] * count,
        out_specs=[IN_VMEM] * count,
        out_shape=[pltpu.VMEM(half, BF16)] * count,
        scratch_shapes=[pltpu.SemaphoreType.DMA((count, len(offsets)))],
        compiler_params=params(36 * MIB),
        cost_estimate=cost(1, 2 * count * depth * width),
    )(me, *weights)


def put(parts, rows, value):
    for i, part in enumerate(parts):
        part[...] = value[i * rows : (i + 1) * rows].astype(BF16)


def resident_kernel(rows_ref, half_ref, *refs):
    sends, keep_ref = refs[-1 - PARTS : -1], refs[-1]
    quarter = keep_ref.shape[2]
    sub = sub_width(quarter)
    for p in range(2):
        for c in range(0, quarter, sub):
            product = jnp.dot(
                rows_ref[...], half_ref[p, :, c : c + sub], preferred_element_type=F32
            )
            if p == 0:
                put([ref.at[:, c : c + sub] for ref in sends], sends[0].shape[0], product)
            else:
                keep_ref[0, :, c : c + sub] = product.astype(BF16)


def result_shapes(count, height, quarter):
    part = jax.ShapeDtypeStruct((height // PARTS, quarter), BF16)
    return [part] * (PARTS * count) + [jax.ShapeDtypeStruct((count, height, quarter), BF16)]


def resident_products(rows, half, after):
    shapes = result_shapes(1, rows.shape[0], half.shape[2])
    *send, keep = pl.pallas_call(
        resident_kernel,
        in_specs=[IN_VMEM] * 2 + [ANYWHERE] * len(after),
        out_specs=[IN_VMEM] * len(shapes),
        out_shape=shapes,
        compiler_params=params(4 * MIB),
        cost_estimate=cost(1, 1),
    )(rows, half, *after)
    return send, keep


def stream_kernel(count, offsets, me_ref, rows_ref, *refs):
    weights, (keep_ref, slots_ref, sems) = refs[:count], refs[-3:]
    sends = refs[-3 - PARTS * count : -3]
    quarter = keep_ref.shape[2]
    slots, unused, sub = slots_ref.shape
    copies, targets = [], []
    for k in range(count):
        for p, offset in enumerate(offsets):
            base = (me_ref[0] ^ offset) * quarter
            for c in range(0, quarter, sub):
                columns = pl.ds(pl.multiple_of(base + c, sub), sub)
                slot = len(copies) % slots
                copies.append(
                    pltpu.make_async_copy(
                        weights[k].at[:, columns], slots_ref.at[slot], sems.at[slot]
                    )
                )
                targets.append((k, p, c))
    for copy in copies[:slots]:
        copy.start()
    for i, (k, p, c) in enumerate(targets):
        copies[i].wait()
        product = jnp.dot(rows_ref[...], slots_ref[i % slots], preferred_element_type=F32)
        if p == 0:
            parts = sends[PARTS * k : PARTS * (k + 1)]
            put([ref.at[:, c : c + sub] for ref in parts], parts[0].shape[0], product)
        else:
            keep_ref[k, :, c : c + sub] = product.astype(BF16)
        if i + slots < len(copies):
            copies[i + slots].start()


def stream_products(me, rows, weights, offsets, after):
    count, (height, depth) = len(weights), rows.shape
    quarter = weights[0].shape[1] // 4
    sub = sub_width(quarter)
    slots = min(4, 2 * count * (quarter // sub))
    shapes = result_shapes(count, height, quarter)
    *send, keep = pl.pallas_call(
        functools.partial(stream_kernel, count, offsets),
        in_specs=[IN_SMEM, IN_VMEM] + [IN_HBM] * count + [ANYWHERE] * len(after),
        out_specs=[IN_VMEM] * len(shapes),
        out_shape=shapes,
        scratch_shapes=[pltpu.VMEM((slots, depth, sub), BF16), pltpu.SemaphoreType.DMA((slots,))],
        compiler_params=params(48 * MIB),
        cost_estimate=cost(1, 1),
    )(me, rows, *weights, *after)
    return send, keep


def stacked(pieces):
    return jnp.concatenate([piece[...].astype(F32) for piece in pieces], axis=0)


def back_kernel(count, jobs, width, me_ref, *refs):
    pieces, weight_ref, turned_ref = refs[:count], refs[count], refs[-1]
    each = 3
    outs = refs[-1 - each * len(jobs) : -1]
    sub = sub_width(width)
    turned_ref[...] = stacked(pieces).T.astype(BF16)
    for job, (offsets, chunk, chunks) in enumerate(jobs):
        sends, keep_ref = outs[each * job : each * job + each - 1], outs[each * job + each - 1]
        height = keep_ref.shape[1]
        for p, offset in enumerate(offsets):
            base = (me_ref[0] ^ offset) * (width * chunks) + chunk * width
            for c in range(0, width, sub):
                piece = weight_ref[pl.ds(pl.multiple_of(base + c, sub), sub), :]
                product = jnp.dot(piece, turned_ref[...], preferred_element_type=F32).T
                if p == 0:
                    put([ref.at[:, c : c + sub] for ref in sends], height, product)
                else:
                    keep_ref[0, :, c : c + sub] = product[:height].astype(BF16)
                    keep_ref[1, :, c : c + sub] = product[height:].astype(BF16)


def back_products(me, pieces, weight, offsets, chunk_list, chunks, after):
    count, (rows, depth) = len(pieces), pieces[0].shape
    height, width = count * rows // 2, weight.shape[0] // (4 * chunks)
    part = jax.ShapeDtypeStruct((height, width), BF16)
    shapes = [part, part, jax.ShapeDtypeStruct((2, height, width), BF16)]
    each = len(shapes)
    jobs = [(offsets, chunk, chunks) for chunk in chunk_list]
    results = pl.pallas_call(
        functools.partial(back_kernel, count, jobs, width),
        in_specs=[IN_SMEM] + [IN_VMEM] * (count + 1) + [ANYWHERE] * len(after),
        out_specs=[IN_VMEM] * (each * len(jobs)),
        out_shape=shapes * len(jobs),
        scratch_shapes=[pltpu.VMEM((depth, 2 * height), BF16)],
        compiler_params=params(8 * MIB),
        cost_estimate=cost(1, 1),
    )(me, *pieces, weight, *after)
    return [
        (results[each * i : each * i + each - 1], results[each * i + each - 1])
        for i in range(len(jobs))
    ]


def down_kernel(offsets, has_start, pieces, me_ref, first_ref, second_ref, weight_ref, *rest):
    outs = rest[-pieces:]
    quarter = first_ref.shape[1]
    width = weight_ref.shape[1]
    sub = sub_width(width)
    for c in range(0, width, sub):
        total = rest[0][:, c : c + sub] if has_start else 0.0
        for rows_ref, offset in zip((first_ref, second_ref), offsets):
            base = pl.multiple_of((me_ref[0] ^ offset) * quarter, quarter)
            piece = weight_ref[pl.ds(base, quarter), c : c + sub]
            total += jnp.dot(rows_ref[...], piece, preferred_element_type=F32)
        for i, out_ref in enumerate(outs):
            rows = out_ref.shape[0]
            out_ref[:, c : c + sub] = total[i * rows : (i + 1) * rows].astype(out_ref.dtype)


def down_products(me, first, second, weight, offsets, start, pieces, out_type, after=()):
    height, quarter = first.shape
    width = weight.shape[1]
    operands = [first, second, weight] + ([] if start is None else [start])
    return pl.pallas_call(
        functools.partial(down_kernel, offsets, start is not None, pieces),
        in_specs=[IN_SMEM] + [IN_VMEM] * len(operands) + [ANYWHERE] * len(after),
        out_specs=[IN_VMEM] * pieces,
        out_shape=[jax.ShapeDtypeStruct((height // pieces, width), out_type)] * pieces,
        compiler_params=params(4 * MIB),
        cost_estimate=cost(1, 1),
    )(me, *operands, *after)


def mix_kernel(count, token_total, *refs):
    pieces, spread_ref, outs = refs[:count], refs[count], refs[-EXPERTS:]
    per_expert = count // EXPERTS
    mixed = 0.0
    for e in range(EXPERTS):
        total = 0.0
        for piece in pieces[e * per_expert : (e + 1) * per_expert]:
            total += piece[...].astype(F32)
        mixed += lax.dot_general(
            spread_ref[e],
            total,
            (((0,), (0,)), ((), ())),
            precision=lax.Precision.HIGHEST,
            preferred_element_type=F32,
        )
    mixed = mixed / token_total
    for e in range(EXPERTS):
        outs[e][...] = jnp.dot(
            spread_ref[e], mixed, precision=lax.Precision.HIGHEST, preferred_element_type=F32
        ).astype(BF16)


def mix_products(pieces, spread, token_total, after=()):
    count = len(pieces)
    result = jax.ShapeDtypeStruct(pieces[0].shape, BF16)
    return pl.pallas_call(
        functools.partial(mix_kernel, count, token_total),
        in_specs=[IN_VMEM] * (count + 1) + [ANYWHERE] * len(after),
        out_specs=[IN_VMEM] * EXPERTS,
        out_shape=[result] * EXPERTS,
        compiler_params=params(8 * MIB),
        cost_estimate=cost(1, 1),
    )(*pieces, spread, *after)


def outer_kernel(places, chunks, flags, me_ref, tokens_ref, *refs):
    terms = refs[: len(places)]
    outs, (turned_ref, slots_ref, sems) = refs[-5:-3], refs[-3:]
    if flags:
        outs = refs[-6:-4]
        refs[-4][...] = jnp.zeros_like(refs[-4])
    width = terms[0].shape[2]
    slots, unused, sub = slots_ref.shape
    turned_ref[...] = tokens_ref[...].astype(F32).T.astype(BF16)
    copies = []
    for term_ref, (offset, chunk) in zip(terms, places):
        base = (me_ref[0] ^ offset) * (width * chunks) + chunk * width
        for k in range(2):
            for c in range(0, width, sub):
                slot = len(copies) % slots
                if len(copies) >= slots:
                    copies[-slots].wait()
                slots_ref[slot] = jnp.dot(
                    turned_ref[...], term_ref[k, :, c : c + sub], preferred_element_type=F32
                ).astype(BF16)
                columns = pl.ds(pl.multiple_of(base + c, sub), sub)
                copy = pltpu.make_async_copy(
                    slots_ref.at[slot], outs[k].at[:, columns], sems.at[slot]
                )
                copy.start()
                copies.append(copy)
    for copy in copies[-slots:]:
        copy.wait()


def outer_products(me, tokens, terms, places, chunks, outputs, after=()):
    height, width = tokens.shape
    columns = terms[0].shape[2]
    sub = sub_width(columns)
    slots = min(4, 2 * len(terms) * (columns // sub))
    operands = [tokens, *terms]
    given = [] if outputs is None else list(outputs)
    flags = int(outputs is None)
    return pl.pallas_call(
        functools.partial(outer_kernel, places, chunks, flags),
        in_specs=[IN_SMEM]
        + [IN_VMEM] * len(operands)
        + [ANYWHERE] * (len(given) + len(after)),
        out_specs=[ANYWHERE] * 2 + [IN_VMEM] * flags,
        out_shape=[jax.ShapeDtypeStruct((width, 4 * chunks * columns), BF16)] * 2
        + [jax.ShapeDtypeStruct((8, 128), F32)] * flags,
        input_output_aliases={1 + len(operands) + k: k for k in range(len(given))},
        scratch_shapes=[
            pltpu.VMEM((width, height), BF16),
            pltpu.VMEM((slots, width, sub), BF16),
            pltpu.SemaphoreType.DMA((slots,)),
        ],
        compiler_params=params(14 * MIB),
        cost_estimate=cost(1, 1),
    )(me, *operands, *given, *after)


def rows_kernel(function, count, results, start_column, *refs):
    ins, outs = refs[:count], refs[-results:]
    height, width = outs[0].shape[-2:]
    for low in range(0, height, ROWS):

        def load(i):
            ref = ins[i]
            if ref.shape[-1] > width:
                return ref[low : low + ROWS, start_column : start_column + width].astype(F32)
            if ref.shape[-2] == height:
                return ref[..., low : low + ROWS, :].astype(F32)
            part, start = divmod(low, ref.shape[-2])
            return ins[i + part][start : start + ROWS].astype(F32)

        for ref, value in zip(outs, function(load)):
            ref[..., low : low + ROWS, :] = value.astype(ref.dtype)


def by_rows(function, operands, shapes, after, start_column=0):
    return pl.pallas_call(
        functools.partial(rows_kernel, function, len(operands), len(shapes), start_column),
        in_specs=[IN_VMEM] * len(operands) + [ANYWHERE] * len(after),
        out_specs=[IN_VMEM] * len(shapes),
        out_shape=[jax.ShapeDtypeStruct(shape, dtype) for shape, dtype in shapes],
        compiler_params=params(12 * MIB),
        cost_estimate=cost(1, 1),
    )(*operands, *after)


def far_rows(load):
    return (load(0)[0] + load(1),)


def far_pair_rows(load):
    near = load(0)
    return (jnp.stack([near[0] + load(1), near[1] + load(2)]),)


def hidden_rows(load):
    near = load(0)
    gate_value = near[0] + load(1) + load(1 + 2 * PARTS)
    up_value = near[1] + load(1 + PARTS) + load(2 + 2 * PARTS)
    return gate_value * jax.nn.sigmoid(gate_value) * up_value, gate_value, up_value


def tangent_rows(load):
    near = load(0)
    gate_tangent = near[0] + load(1) + load(1 + 2 * PARTS)
    up_tangent = near[1] + load(1 + PARTS) + load(2 + 2 * PARTS)
    gate_value, up_value = load(3 + 2 * PARTS), load(4 + 2 * PARTS)
    s = jax.nn.sigmoid(gate_value)
    slope = s + gate_value * s * (1.0 - s)
    hidden_tangent = slope * gate_tangent * up_value + gate_value * s * up_tangent
    return hidden_tangent, gate_tangent, up_tangent


def term_rows(load):
    near, across = load(0), load(1)
    back_value = near[0] + load(2) + across[0]
    back_tangent = near[1] + load(3) + across[1]
    gate_value, up_value, gate_tangent, up_tangent = (load(4 + i) for i in range(4))
    s = jax.nn.sigmoid(gate_value)
    slope = s + gate_value * s * (1.0 - s)
    bend = s * (1.0 - s) * (2.0 + gate_value * (1.0 - 2.0 * s))
    gate_term = (
        back_tangent * up_value * slope
        + back_value * up_tangent * slope
        + back_value * up_value * bend * gate_tangent
    )
    up_term = back_tangent * (gate_value * s) + back_value * slope * gate_tangent
    return (jnp.stack([gate_term, up_term]),)


def pass_kernel(value_ref, *refs):
    refs[-1][...] = value_ref[...]


def pass_on(value, after):
    return pl.pallas_call(
        pass_kernel,
        in_specs=[IN_VMEM] + [ANYWHERE] * len(after),
        out_specs=IN_VMEM,
        out_shape=jax.ShapeDtypeStruct(value.shape, value.dtype),
        compiler_params=params(4 * MIB),
        cost_estimate=cost(1, 1),
    )(value, *after)


def exchange(pieces):
    ranks = lax.axis_size("expert")
    if ranks <= 4:
        return [pieces[0]] + [swap(pieces[i], "expert", i) for i in range(1, ranks)]
    order = lax.axis_index("expert") ^ jnp.arange(ranks)
    stacked = jnp.take(jnp.stack(pieces), order, axis=0)
    moved = lax.all_to_all(stacked, "expert", split_axis=0, concat_axis=0, tiled=True)
    moved = jnp.take(moved, order, axis=0)
    return [moved[i] for i in range(ranks)]


def routing_tables(expert_ids, route_weights, expert_list, capacity):
    matches = expert_ids[None, :, :] == expert_list[:, None, None]
    chosen = jnp.any(matches, axis=2)
    route_share = jnp.sum(jnp.where(matches, route_weights[None, :, :], F32(0.0)), axis=2)
    place = jnp.cumsum(chosen.astype(jnp.int32), axis=1) - 1
    slot_ids = jnp.arange(capacity, dtype=jnp.int32)
    route_table = chosen[:, None, :] & (place[:, None, :] == slot_ids[None, :, None])
    return route_table, route_share


def per_device(
    tokens, expert_ids, route_weights, gate_weight, up_weight, down_weight, gate_probe, up_probe
):
    tok_rows, width_dev = tokens.shape
    capacity = tok_rows // 2
    ranks = lax.axis_size("expert")
    per_expert = ranks // EXPERTS
    token_total = ranks * tok_rows
    me = lax.axis_index("dp").astype(jnp.int32).reshape(1)
    mine = lax.axis_index("expert") // per_expert
    expert_list = jnp.stack([mine, 1 - mine]).astype(expert_ids.dtype)

    route_table, route_share = routing_tables(expert_ids, route_weights, expert_list, capacity)
    spread = route_table.astype(F32) * route_share[:, None, :]
    slots = jnp.einsum(
        "ect,tf->ecf", route_table.astype(BF16), tokens, preferred_element_type=F32
    ).astype(BF16)
    slot_rows = jnp.concatenate(exchange([slots[i // per_expert] for i in range(ranks)]), axis=0)

    def core(parts):
        return [swap(part, "dp", 1) for part in parts]

    height, quarter = slot_rows.shape[0], down_weight.shape[0] // 4
    part_type = ((height, quarter), BF16)
    wide_type = ((height, quarter), F32)

    def far_sum(keep, got, after):
        (far,) = by_rows(far_rows, [keep, *got], [part_type], after)
        return far, swap(far, "dp", 2)

    halves = prefetch(me, [gate_weight, up_weight, gate_probe], (3, 2))
    send, keep = resident_products(slot_rows, halves[0], [])
    gate_far = (keep, core(send))
    send, keep = resident_products(slot_rows, halves[1], [keep])
    up_far = (keep, core(send))
    far, gate_across = far_sum(*gate_far, [keep])
    send, keep = resident_products(slot_rows, halves[2], [far])
    gate_tangent_far = (keep, core(send))
    far, up_across = far_sum(*up_far, [keep])
    send, near = stream_products(me, slot_rows, [gate_weight, up_weight], (1, 0), [far])
    near_got = core(send)
    far, gate_tangent_across = far_sum(*gate_tangent_far, [near, gate_across])
    hidden, gate_value, up_value = by_rows(
        hidden_rows,
        [near, *near_got, gate_across, up_across],
        [part_type, wide_type, wide_type],
        [far],
    )
    beside, across = swap(hidden, "dp", 1), swap(hidden, "dp", 2)
    send, keep = stream_products(me, slot_rows, [up_probe], (3, 2), [hidden])
    got = core(send)
    (half_value,) = down_products(
        me, hidden, beside, down_weight, (0, 1), None, 1, F32, [keep]
    )
    far, up_tangent_across = far_sum(keep, got, [half_value])
    send, near_tangent = stream_products(
        me, slot_rows, [gate_probe, up_probe], (1, 0), [far, gate_tangent_across]
    )
    got = core(send)
    hidden_tangent, gate_tangent, up_tangent = by_rows(
        tangent_rows,
        [
            near_tangent,
            *got,
            gate_tangent_across,
            up_tangent_across,
            gate_value,
            up_value,
        ],
        [part_type, wide_type, wide_type],
        [],
    )
    out = down_products(
        me,
        across,
        swap(across, "dp", 1),
        down_weight,
        (2, 3),
        half_value,
        ranks,
        BF16,
        [hidden_tangent],
    )
    came = exchange(out)

    beside, across = swap(hidden_tangent, "dp", 1), swap(hidden_tangent, "dp", 2)
    (half,) = down_products(
        me, hidden_tangent, beside, down_weight, (0, 1), None, 1, F32, [out[0]]
    )
    across = pass_on(across, [half, came[1]])
    out = down_products(
        me, across, swap(across, "dp", 1), down_weight, (2, 3), half, ranks, BF16, []
    )
    came_tangent = exchange(out)
    cot = mix_products(came, spread, token_total, [out[0], came_tangent[1]])
    came = exchange([cot[i // per_expert] for i in range(ranks)])
    cot = mix_products(came_tangent, spread, token_total, [cot[0], came[1]])
    came += exchange([cot[i // per_expert] for i in range(ranks)])

    chunks = 2 if quarter % 256 == 0 else 1
    width = quarter // chunks
    pair_type = ((2, height, width), BF16)
    keep, ends = cot[0], []
    for i in range(chunks):
        ((send, keep),) = back_products(me, came, down_weight, (3, 2), [i], chunks, [keep])
        ends.append((keep, core(send)))
    fars = []
    for i in range(chunks - 1):
        fars += by_rows(far_pair_rows, [ends[i][0], *ends[i][1]], [pair_type], [keep])
    nears = back_products(me, came, down_weight, (1, 0), range(chunks), chunks, fars + [keep])
    fars += by_rows(far_pair_rows, [ends[-1][0], *ends[-1][1]], [pair_type], [nears[0][1]])
    sums = [swap(far, "dp", 2) for far in fars]
    nears = [[keep, *core(send)] for send, keep in nears]

    last, terms = fars[-1], []
    for i in range(chunks):
        (near, *got) = nears[i]
        terms += by_rows(
            term_rows,
            [near, sums[i], *got, gate_value, up_value, gate_tangent, up_tangent],
            [pair_type],
            [last],
            i * width,
        )
        last = terms[-1]
    across = [swap(term, "dp", 2) for term in terms]
    beside = [swap(term, "dp", 1) for term in terms]
    places = [(offset, i) for offset in (0, 1) for i in range(chunks)]
    *outputs, last = outer_products(
        me, slot_rows, terms + beside, places, chunks, None, across[: chunks - 1]
    )
    last = pass_on(across[-1], [last])
    passed = [(part, swap(part, "dp", 1)) for part in across[:-1] + [last]]
    for i in range(chunks):
        outputs = outer_products(
            me, slot_rows, passed[i], [(2, i), (3, i)], chunks, outputs, [last]
        )
    return tuple(outputs)


def solution(mesh):
    return jax.shard_map(
        per_device,
        mesh=mesh,
        in_specs=(
            P(("groups", "expert"), "dp"),
            P(("groups", "expert"), None),
            P(("groups", "expert"), None),
            P("dp", "expert"),
            P("dp", "expert"),
            P("expert", "dp"),
            P("dp", "expert"),
            P("dp", "expert"),
        ),
        out_specs=(P(("groups", "dp"), "expert"), P(("groups", "dp"), "expert")),
        check_vma=False,
    )
```

```python
import functools

import jax
import jax.numpy as jnp
from jax import lax
from jax.experimental import pallas as pl
from jax.experimental.pallas import tpu as pltpu
from jax.sharding import PartitionSpec as P

EXPERTS = 2
BF16 = jnp.bfloat16
F32 = jnp.float32
KIB = 1024
MIB = 1024 * KIB
IN_VMEM = pl.BlockSpec(memory_space=pltpu.VMEM)
IN_SMEM = pl.BlockSpec(memory_space=pltpu.SMEM)
IN_HBM = pl.BlockSpec(memory_space=pltpu.HBM)
ANYWHERE = pl.BlockSpec(memory_space=pl.ANY)
PARTS = 2
ROWS = 16


def swap(value, axis, mask):
    size = lax.axis_size(axis)
    return lax.ppermute(value, axis, [(i, i ^ mask) for i in range(size)])


def sub_width(width):
    return 512 if width % 512 == 0 else width


def params(limit):
    return pltpu.CompilerParams(vmem_limit_bytes=limit)


def cost(flops, size):
    return pl.CostEstimate(flops=flops, bytes_accessed=size, transcendentals=0)


def prefetch_kernel(offsets, me_ref, *refs):
    weights, halves, sems = refs[: (len(refs) - 1) // 2], refs[(len(refs) - 1) // 2 : -1], refs[-1]
    quarter = halves[0].shape[2]
    copies = []
    for k, (weight_ref, half_ref) in enumerate(zip(weights, halves)):
        for p, offset in enumerate(offsets):
            base = pl.multiple_of((me_ref[0] ^ offset) * quarter, quarter)
            copies.append(
                pltpu.make_async_copy(
                    weight_ref.at[:, pl.ds(base, quarter)], half_ref.at[p], sems.at[k, p]
                )
            )
    for copy in copies:
        copy.start()
    for copy in copies:
        copy.wait()


def prefetch(me, weights, offsets):
    count, (depth, width) = len(weights), weights[0].shape
    half = (len(offsets), depth, width // 4)
    return pl.pallas_call(
        functools.partial(prefetch_kernel, offsets),
        in_specs=[IN_SMEM] + [IN_HBM] * count,
        out_specs=[IN_VMEM] * count,
        out_shape=[pltpu.VMEM(half, BF16)] * count,
        scratch_shapes=[pltpu.SemaphoreType.DMA((count, len(offsets)))],
        compiler_params=params(36 * MIB),
        cost_estimate=cost(1, 2 * count * depth * width),
    )(me, *weights)


def put(parts, rows, value):
    for i, part in enumerate(parts):
        part[...] = value[i * rows : (i + 1) * rows].astype(BF16)


def resident_kernel(rows_ref, half_ref, *refs):
    sends, keep_ref = refs[-1 - PARTS : -1], refs[-1]
    quarter = keep_ref.shape[2]
    sub = sub_width(quarter)
    for p in range(2):
        for c in range(0, quarter, sub):
            product = jnp.dot(
                rows_ref[...], half_ref[p, :, c : c + sub], preferred_element_type=F32
            )
            if p == 0:
                put([ref.at[:, c : c + sub] for ref in sends], sends[0].shape[0], product)
            else:
                keep_ref[0, :, c : c + sub] = product.astype(BF16)


def result_shapes(count, height, quarter):
    part = jax.ShapeDtypeStruct((height // PARTS, quarter), BF16)
    return [part] * (PARTS * count) + [jax.ShapeDtypeStruct((count, height, quarter), BF16)]


def resident_products(rows, half, after):
    shapes = result_shapes(1, rows.shape[0], half.shape[2])
    *send, keep = pl.pallas_call(
        resident_kernel,
        in_specs=[IN_VMEM] * 2 + [ANYWHERE] * len(after),
        out_specs=[IN_VMEM] * len(shapes),
        out_shape=shapes,
        compiler_params=params(4 * MIB),
        cost_estimate=cost(1, 1),
    )(rows, half, *after)
    return send, keep


def stream_kernel(count, offsets, me_ref, rows_ref, *refs):
    weights, (keep_ref, slots_ref, sems) = refs[:count], refs[-3:]
    sends = refs[-3 - PARTS * count : -3]
    quarter = keep_ref.shape[2]
    slots, unused, sub = slots_ref.shape
    copies, targets = [], []
    for k in range(count):
        for p, offset in enumerate(offsets):
            base = (me_ref[0] ^ offset) * quarter
            for c in range(0, quarter, sub):
                columns = pl.ds(pl.multiple_of(base + c, sub), sub)
                slot = len(copies) % slots
                copies.append(
                    pltpu.make_async_copy(
                        weights[k].at[:, columns], slots_ref.at[slot], sems.at[slot]
                    )
                )
                targets.append((k, p, c))
    for copy in copies[:slots]:
        copy.start()
    for i, (k, p, c) in enumerate(targets):
        copies[i].wait()
        product = jnp.dot(rows_ref[...], slots_ref[i % slots], preferred_element_type=F32)
        if p == 0:
            parts = sends[PARTS * k : PARTS * (k + 1)]
            put([ref.at[:, c : c + sub] for ref in parts], parts[0].shape[0], product)
        else:
            keep_ref[k, :, c : c + sub] = product.astype(BF16)
        if i + slots < len(copies):
            copies[i + slots].start()


def stream_products(me, rows, weights, offsets, after):
    count, (height, depth) = len(weights), rows.shape
    quarter = weights[0].shape[1] // 4
    sub = sub_width(quarter)
    slots = min(8, 2 * count * (quarter // sub))
    shapes = result_shapes(count, height, quarter)
    *send, keep = pl.pallas_call(
        functools.partial(stream_kernel, count, offsets),
        in_specs=[IN_SMEM, IN_VMEM] + [IN_HBM] * count + [ANYWHERE] * len(after),
        out_specs=[IN_VMEM] * len(shapes),
        out_shape=shapes,
        scratch_shapes=[pltpu.VMEM((slots, depth, sub), BF16), pltpu.SemaphoreType.DMA((slots,))],
        compiler_params=params(48 * MIB),
        cost_estimate=cost(1, 1),
    )(me, rows, *weights, *after)
    return send, keep


def stacked(pieces):
    return jnp.concatenate([piece[...].astype(F32) for piece in pieces], axis=0)


def back_kernel(count, jobs, width, me_ref, *refs):
    pieces, weight_ref, turned_ref = refs[:count], refs[count], refs[-1]
    each = 3
    outs = refs[-1 - each * len(jobs) : -1]
    sub = sub_width(width)
    turned_ref[...] = stacked(pieces).T.astype(BF16)
    for job, (offsets, chunk, chunks) in enumerate(jobs):
        sends, keep_ref = outs[each * job : each * job + each - 1], outs[each * job + each - 1]
        height = keep_ref.shape[1]
        for p, offset in enumerate(offsets):
            base = (me_ref[0] ^ offset) * (width * chunks) + chunk * width
            for c in range(0, width, sub):
                piece = weight_ref[pl.ds(pl.multiple_of(base + c, sub), sub), :]
                product = jnp.dot(piece, turned_ref[...], preferred_element_type=F32).T
                if p == 0:
                    put([ref.at[:, c : c + sub] for ref in sends], height, product)
                else:
                    keep_ref[0, :, c : c + sub] = product[:height].astype(BF16)
                    keep_ref[1, :, c : c + sub] = product[height:].astype(BF16)


def back_products(me, pieces, weight, offsets, chunk_list, chunks, after):
    count, (rows, depth) = len(pieces), pieces[0].shape
    height, width = count * rows // 2, weight.shape[0] // (4 * chunks)
    part = jax.ShapeDtypeStruct((height, width), BF16)
    shapes = [part, part, jax.ShapeDtypeStruct((2, height, width), BF16)]
    each = len(shapes)
    jobs = [(offsets, chunk, chunks) for chunk in chunk_list]
    results = pl.pallas_call(
        functools.partial(back_kernel, count, jobs, width),
        in_specs=[IN_SMEM] + [IN_VMEM] * (count + 1) + [ANYWHERE] * len(after),
        out_specs=[IN_VMEM] * (each * len(jobs)),
        out_shape=shapes * len(jobs),
        scratch_shapes=[pltpu.VMEM((depth, 2 * height), BF16)],
        compiler_params=params(8 * MIB),
        cost_estimate=cost(1, 1),
    )(me, *pieces, weight, *after)
    return [
        (results[each * i : each * i + each - 1], results[each * i + each - 1])
        for i in range(len(jobs))
    ]


def down_kernel(offsets, has_start, pieces, me_ref, first_ref, second_ref, weight_ref, *rest):
    outs = rest[-pieces:]
    quarter = first_ref.shape[1]
    width = weight_ref.shape[1]
    sub = sub_width(width)
    for c in range(0, width, sub):
        total = rest[0][:, c : c + sub] if has_start else 0.0
        for rows_ref, offset in zip((first_ref, second_ref), offsets):
            base = pl.multiple_of((me_ref[0] ^ offset) * quarter, quarter)
            piece = weight_ref[pl.ds(base, quarter), c : c + sub]
            total += jnp.dot(rows_ref[...], piece, preferred_element_type=F32)
        for i, out_ref in enumerate(outs):
            rows = out_ref.shape[0]
            out_ref[:, c : c + sub] = total[i * rows : (i + 1) * rows].astype(out_ref.dtype)


def down_products(me, first, second, weight, offsets, start, pieces, out_type, after=()):
    height, quarter = first.shape
    width = weight.shape[1]
    operands = [first, second, weight] + ([] if start is None else [start])
    return pl.pallas_call(
        functools.partial(down_kernel, offsets, start is not None, pieces),
        in_specs=[IN_SMEM] + [IN_VMEM] * len(operands) + [ANYWHERE] * len(after),
        out_specs=[IN_VMEM] * pieces,
        out_shape=[jax.ShapeDtypeStruct((height // pieces, width), out_type)] * pieces,
        compiler_params=params(4 * MIB),
        cost_estimate=cost(1, 1),
    )(me, *operands, *after)


def mix_kernel(count, token_total, *refs):
    pieces, spread_ref, outs = refs[:count], refs[count], refs[-EXPERTS:]
    per_expert = count // EXPERTS
    mixed = 0.0
    for e in range(EXPERTS):
        total = 0.0
        for piece in pieces[e * per_expert : (e + 1) * per_expert]:
            total += piece[...].astype(F32)
        mixed += lax.dot_general(
            spread_ref[e],
            total,
            (((0,), (0,)), ((), ())),
            precision=lax.Precision.HIGHEST,
            preferred_element_type=F32,
        )
    mixed = mixed / token_total
    for e in range(EXPERTS):
        outs[e][...] = jnp.dot(
            spread_ref[e], mixed, precision=lax.Precision.HIGHEST, preferred_element_type=F32
        ).astype(BF16)


def mix_products(pieces, spread, token_total, after=()):
    count = len(pieces)
    result = jax.ShapeDtypeStruct(pieces[0].shape, BF16)
    return pl.pallas_call(
        functools.partial(mix_kernel, count, token_total),
        in_specs=[IN_VMEM] * (count + 1) + [ANYWHERE] * len(after),
        out_specs=[IN_VMEM] * EXPERTS,
        out_shape=[result] * EXPERTS,
        compiler_params=params(8 * MIB),
        cost_estimate=cost(1, 1),
    )(*pieces, spread, *after)


def outer_kernel(places, chunks, flags, me_ref, tokens_ref, *refs):
    terms = refs[: len(places)]
    outs, (turned_ref, slots_ref, sems) = refs[-5:-3], refs[-3:]
    if flags:
        outs = refs[-6:-4]
        refs[-4][...] = jnp.zeros_like(refs[-4])
    width = terms[0].shape[2]
    slots, unused, sub = slots_ref.shape
    turned_ref[...] = tokens_ref[...].astype(F32).T.astype(BF16)
    copies = []
    for term_ref, (offset, chunk) in zip(terms, places):
        base = (me_ref[0] ^ offset) * (width * chunks) + chunk * width
        for k in range(2):
            for c in range(0, width, sub):
                slot = len(copies) % slots
                if len(copies) >= slots:
                    copies[-slots].wait()
                slots_ref[slot] = jnp.dot(
                    turned_ref[...], term_ref[k, :, c : c + sub], preferred_element_type=F32
                ).astype(BF16)
                columns = pl.ds(pl.multiple_of(base + c, sub), sub)
                copy = pltpu.make_async_copy(
                    slots_ref.at[slot], outs[k].at[:, columns], sems.at[slot]
                )
                copy.start()
                copies.append(copy)
    for copy in copies[-slots:]:
        copy.wait()


def outer_products(me, tokens, terms, places, chunks, outputs, after=()):
    height, width = tokens.shape
    columns = terms[0].shape[2]
    sub = sub_width(columns)
    slots = min(4, 2 * len(terms) * (columns // sub))
    operands = [tokens, *terms]
    given = [] if outputs is None else list(outputs)
    flags = int(outputs is None)
    return pl.pallas_call(
        functools.partial(outer_kernel, places, chunks, flags),
        in_specs=[IN_SMEM]
        + [IN_VMEM] * len(operands)
        + [ANYWHERE] * (len(given) + len(after)),
        out_specs=[ANYWHERE] * 2 + [IN_VMEM] * flags,
        out_shape=[jax.ShapeDtypeStruct((width, 4 * chunks * columns), BF16)] * 2
        + [jax.ShapeDtypeStruct((8, 128), F32)] * flags,
        input_output_aliases={1 + len(operands) + k: k for k in range(len(given))},
        scratch_shapes=[
            pltpu.VMEM((width, height), BF16),
            pltpu.VMEM((slots, width, sub), BF16),
            pltpu.SemaphoreType.DMA((slots,)),
        ],
        compiler_params=params(14 * MIB),
        cost_estimate=cost(1, 1),
    )(me, *operands, *given, *after)


def rows_kernel(function, count, results, start_column, *refs):
    ins, outs = refs[:count], refs[-results:]
    height, width = outs[0].shape[-2:]
    for low in range(0, height, ROWS):

        def load(i):
            ref = ins[i]
            if ref.shape[-1] > width:
                return ref[low : low + ROWS, start_column : start_column + width].astype(F32)
            if ref.shape[-2] == height:
                return ref[..., low : low + ROWS, :].astype(F32)
            part, start = divmod(low, ref.shape[-2])
            return ins[i + part][start : start + ROWS].astype(F32)

        for ref, value in zip(outs, function(load)):
            ref[..., low : low + ROWS, :] = value.astype(ref.dtype)


def by_rows(function, operands, shapes, after, start_column=0):
    return pl.pallas_call(
        functools.partial(rows_kernel, function, len(operands), len(shapes), start_column),
        in_specs=[IN_VMEM] * len(operands) + [ANYWHERE] * len(after),
        out_specs=[IN_VMEM] * len(shapes),
        out_shape=[jax.ShapeDtypeStruct(shape, dtype) for shape, dtype in shapes],
        compiler_params=params(12 * MIB),
        cost_estimate=cost(1, 1),
    )(*operands, *after)


def far_rows(load):
    return (load(0)[0] + load(1),)


def far_pair_rows(load):
    near = load(0)
    return (jnp.stack([near[0] + load(1), near[1] + load(2)]),)


def hidden_rows(load):
    near = load(0)
    gate_value = near[0] + load(1) + load(1 + 2 * PARTS)
    up_value = near[1] + load(1 + PARTS) + load(2 + 2 * PARTS)
    return gate_value * jax.nn.sigmoid(gate_value) * up_value, gate_value, up_value


def tangent_rows(load):
    near = load(0)
    gate_tangent = near[0] + load(1) + load(1 + 2 * PARTS)
    up_tangent = near[1] + load(1 + PARTS) + load(2 + 2 * PARTS)
    gate_value, up_value = load(3 + 2 * PARTS), load(4 + 2 * PARTS)
    s = jax.nn.sigmoid(gate_value)
    slope = s + gate_value * s * (1.0 - s)
    hidden_tangent = slope * gate_tangent * up_value + gate_value * s * up_tangent
    return hidden_tangent, gate_tangent, up_tangent


def term_rows(load):
    near, across = load(0), load(1)
    back_value = near[0] + load(2) + across[0]
    back_tangent = near[1] + load(3) + across[1]
    gate_value, up_value, gate_tangent, up_tangent = (load(4 + i) for i in range(4))
    s = jax.nn.sigmoid(gate_value)
    slope = s + gate_value * s * (1.0 - s)
    bend = s * (1.0 - s) * (2.0 + gate_value * (1.0 - 2.0 * s))
    gate_term = (
        back_tangent * up_value * slope
        + back_value * up_tangent * slope
        + back_value * up_value * bend * gate_tangent
    )
    up_term = back_tangent * (gate_value * s) + back_value * slope * gate_tangent
    return (jnp.stack([gate_term, up_term]),)


def pass_kernel(value_ref, *refs):
    refs[-1][...] = value_ref[...]


def pass_on(value, after):
    return pl.pallas_call(
        pass_kernel,
        in_specs=[IN_VMEM] + [ANYWHERE] * len(after),
        out_specs=IN_VMEM,
        out_shape=jax.ShapeDtypeStruct(value.shape, value.dtype),
        compiler_params=params(4 * MIB),
        cost_estimate=cost(1, 1),
    )(value, *after)


def exchange(pieces):
    ranks = lax.axis_size("expert")
    if ranks <= 4:
        return [pieces[0]] + [swap(pieces[i], "expert", i) for i in range(1, ranks)]
    order = lax.axis_index("expert") ^ jnp.arange(ranks)
    stacked = jnp.take(jnp.stack(pieces), order, axis=0)
    moved = lax.all_to_all(stacked, "expert", split_axis=0, concat_axis=0, tiled=True)
    moved = jnp.take(moved, order, axis=0)
    return [moved[i] for i in range(ranks)]


def routing_tables(expert_ids, route_weights, expert_list, capacity):
    matches = expert_ids[None, :, :] == expert_list[:, None, None]
    chosen = jnp.any(matches, axis=2)
    route_share = jnp.sum(jnp.where(matches, route_weights[None, :, :], F32(0.0)), axis=2)
    place = jnp.cumsum(chosen.astype(jnp.int32), axis=1) - 1
    slot_ids = jnp.arange(capacity, dtype=jnp.int32)
    route_table = chosen[:, None, :] & (place[:, None, :] == slot_ids[None, :, None])
    return route_table, route_share


def per_device(
    tokens, expert_ids, route_weights, gate_weight, up_weight, down_weight, gate_probe, up_probe
):
    tok_rows, width_dev = tokens.shape
    capacity = tok_rows // 2
    ranks = lax.axis_size("expert")
    per_expert = ranks // EXPERTS
    token_total = ranks * tok_rows
    me = lax.axis_index("dp").astype(jnp.int32).reshape(1)
    mine = lax.axis_index("expert") // per_expert
    expert_list = jnp.stack([mine, 1 - mine]).astype(expert_ids.dtype)

    route_table, route_share = routing_tables(expert_ids, route_weights, expert_list, capacity)
    spread = route_table.astype(F32) * route_share[:, None, :]
    slots = jnp.einsum(
        "ect,tf->ecf", route_table.astype(BF16), tokens, preferred_element_type=F32
    ).astype(BF16)
    slot_rows = jnp.concatenate(exchange([slots[i // per_expert] for i in range(ranks)]), axis=0)

    def core(parts):
        return [swap(part, "dp", 1) for part in parts]

    height, quarter = slot_rows.shape[0], down_weight.shape[0] // 4
    part_type = ((height, quarter), BF16)
    wide_type = ((height, quarter), F32)

    def far_sum(keep, got, after):
        (far,) = by_rows(far_rows, [keep, *got], [part_type], after)
        return far, swap(far, "dp", 2)

    halves = prefetch(me, [gate_weight, up_weight, gate_probe], (3, 2))
    send, keep = resident_products(slot_rows, halves[0], [])
    gate_far = (keep, core(send))
    send, keep = resident_products(slot_rows, halves[1], [keep])
    up_far = (keep, core(send))
    far, gate_across = far_sum(*gate_far, [keep])
    send, keep = resident_products(slot_rows, halves[2], [far])
    gate_tangent_far = (keep, core(send))
    far, up_across = far_sum(*up_far, [keep])
    send, near = stream_products(me, slot_rows, [gate_weight, up_weight], (1, 0), [far])
    near_got = core(send)
    far, gate_tangent_across = far_sum(*gate_tangent_far, [near, gate_across])
    hidden, gate_value, up_value = by_rows(
        hidden_rows,
        [near, *near_got, gate_across, up_across],
        [part_type, wide_type, wide_type],
        [far],
    )
    beside, across = swap(hidden, "dp", 1), swap(hidden, "dp", 2)
    send, keep = stream_products(me, slot_rows, [up_probe], (3, 2), [hidden])
    got = core(send)
    (half_value,) = down_products(
        me, hidden, beside, down_weight, (0, 1), None, 1, F32, [keep]
    )
    far, up_tangent_across = far_sum(keep, got, [half_value])
    send, near_tangent = stream_products(
        me, slot_rows, [gate_probe, up_probe], (1, 0), [far, gate_tangent_across]
    )
    got = core(send)
    hidden_tangent, gate_tangent, up_tangent = by_rows(
        tangent_rows,
        [
            near_tangent,
            *got,
            gate_tangent_across,
            up_tangent_across,
            gate_value,
            up_value,
        ],
        [part_type, wide_type, wide_type],
        [],
    )
    out = down_products(
        me,
        across,
        swap(across, "dp", 1),
        down_weight,
        (2, 3),
        half_value,
        ranks,
        BF16,
        [hidden_tangent],
    )
    came = exchange(out)

    beside, across = swap(hidden_tangent, "dp", 1), swap(hidden_tangent, "dp", 2)
    (half,) = down_products(
        me, hidden_tangent, beside, down_weight, (0, 1), None, 1, F32, [out[0]]
    )
    across = pass_on(across, [half, came[1]])
    out = down_products(
        me, across, swap(across, "dp", 1), down_weight, (2, 3), half, ranks, BF16, []
    )
    came_tangent = exchange(out)
    cot = mix_products(came, spread, token_total, [out[0], came_tangent[1]])
    came = exchange([cot[i // per_expert] for i in range(ranks)])
    cot = mix_products(came_tangent, spread, token_total, [cot[0], came[1]])
    came += exchange([cot[i // per_expert] for i in range(ranks)])

    chunks = 2 if quarter % 256 == 0 else 1
    width = quarter // chunks
    pair_type = ((2, height, width), BF16)
    keep, ends = cot[0], []
    for i in range(chunks):
        ((send, keep),) = back_products(me, came, down_weight, (3, 2), [i], chunks, [keep])
        ends.append((keep, core(send)))
    fars = []
    for i in range(chunks - 1):
        fars += by_rows(far_pair_rows, [ends[i][0], *ends[i][1]], [pair_type], [keep])
    nears = back_products(me, came, down_weight, (1, 0), range(chunks), chunks, fars + [keep])
    fars += by_rows(far_pair_rows, [ends[-1][0], *ends[-1][1]], [pair_type], [nears[0][1]])
    sums = [swap(far, "dp", 2) for far in fars]
    nears = [[keep, *core(send)] for send, keep in nears]

    last, terms = fars[-1], []
    for i in range(chunks):
        (near, *got) = nears[i]
        terms += by_rows(
            term_rows,
            [near, sums[i], *got, gate_value, up_value, gate_tangent, up_tangent],
            [pair_type],
            [last],
            i * width,
        )
        last = terms[-1]
    across = [swap(term, "dp", 2) for term in terms]
    beside = [swap(term, "dp", 1) for term in terms]
    places = [(offset, i) for offset in (0, 1) for i in range(chunks)]
    *outputs, last = outer_products(
        me, slot_rows, terms + beside, places, chunks, None, across[: chunks - 1]
    )
    last = pass_on(across[-1], [last])
    passed = [(part, swap(part, "dp", 1)) for part in across[:-1] + [last]]
    for i in range(chunks):
        outputs = outer_products(
            me, slot_rows, passed[i], [(2, i), (3, i)], chunks, outputs, [last]
        )
    return tuple(outputs)


def solution(mesh):
    return jax.shard_map(
        per_device,
        mesh=mesh,
        in_specs=(
            P(("groups", "expert"), "dp"),
            P(("groups", "expert"), None),
            P(("groups", "expert"), None),
            P("dp", "expert"),
            P("dp", "expert"),
            P("expert", "dp"),
            P("dp", "expert"),
            P("dp", "expert"),
        ),
        out_specs=(P(("groups", "dp"), "expert"), P(("groups", "dp"), "expert")),
        check_vma=False,
    )
```
